128 devices in a mesh: seq: 8 (over z, core), batch: 16 (over x, y).
Axes of the slice: x: 4, y: 4, z: 4, core: 2. Of those that a mesh axis runs over, the one named last changes fastest.
Arguments:
- queries: bfloat16 [16, 4096, 2048], P('batch', 'seq'), may hold values from -6 to 6
- keys: bfloat16 [16, 4096, 2048], P('batch', 'seq'), may hold values from -6 to 6
- values: bfloat16 [16, 4096, 2048], P('batch', 'seq'), may hold values from -6 to 6
- level_gain: float32 [16, 4096, 128], P('batch', 'seq'), may hold values from 0.004 to 0.06
- out_weight: bfloat16 [2048, 2048], P('batch'), may hold values from -0.125 to 0.125
- out_grad: bfloat16 [16, 4096, 2048], P('batch', 'seq'), may hold values from -6 to 6
Outputs:
- query_grad: bfloat16 [16, 4096, 2048], P('batch', 'seq')
- key_grad: bfloat16 [16, 4096, 2048], P('batch', 'seq')
- value_grad: bfloat16 [16, 4096, 2048], P('batch', 'seq')
- gain_grad: float32 [16, 4096, 128], P('batch', 'seq')
- weight_grad: float32 [2048, 2048], P(('seq', 'batch'))
The draws below stay inside these ranges and needn't reach their ends.
All inputs are finite; a program needn't handle non-finite values.
Results may differ from the reference program's by a relative error of at most 0.0064.
Values may be sent and summed in bfloat16 or wider, within the bound.
A program may use at most 192 MiB of HBM per device.

```python
import math
import jax
import jax.numpy as jnp
import numpy as np
from jax import lax

H = 16
HD = 128
D = 2048
TOK_DEV = 512
GROUP = 64
LEVELS = 8
TOKENS = 4096
BATCH = 16
N_SEQ = 8


def shard_levels(own_key, shape, shards, least, top_value):
    factor_of, own = 1.0, jax.random.fold_in(own_key, 6)
    for axis_at, shards_of in shards:
        heights = jnp.exp(jax.random.uniform(jax.random.fold_in(own, axis_at), (shards_of,), jnp.float32, least / len(shards), top_value / len(shards)))
        factor_of = factor_of * jnp.repeat(heights, shape[axis_at] // shards_of).reshape([-1 if axis == axis_at else 1 for axis in range(len(shape))])
    return factor_of


def normal_values(key, dims, spread, limit, shards=(), held_as=jnp.bfloat16):
    loudness = shard_levels(key, dims, shards, -0.22, 0.18) if shards else 1.0
    values = jax.random.normal(key, dims, jnp.float32) * spread * loudness
    return jnp.minimum(jnp.maximum(values, -limit), limit).astype(held_as)


def setup_inputs(seed: int = 0) -> dict:
    seeds = jax.random.split(jax.random.key(seed), 7)
    return {
        "queries": normal_values(seeds[0], (BATCH, TOKENS, D), 1.0, 6.0, ((0, 16), (1, 8))),
        "keys": normal_values(seeds[1], (BATCH, TOKENS, D), 1.0, 6.0, ((0, 16), (1, 8))),
        "values": normal_values(seeds[2], (BATCH, TOKENS, D), 1.0, 6.0, ((0, 16), (1, 8))),
        "level_gain": jnp.clip(jnp.exp(math.log(0.06) - 2.70805 * jax.random.uniform(seeds[3], (BATCH, TOKENS, LEVELS * H), jnp.float32) ** shard_levels(seeds[3], (BATCH, TOKENS, LEVELS * H), ((0, 16), (1, 8)), -0.2, 0.2)), 0.004, 0.06),
        "out_weight": normal_values(seeds[4], (D, D), D ** -0.5, 0.125, ((0, 16),)),
        "out_grad": normal_values(seeds[5], (BATCH, TOKENS, D), 1.0, 6.0, ((0, 16), (1, 8))),
    }


def level_selects(seg_len):
    loc_bits = (seg_len // GROUP).bit_length() - 1
    position = np.arange(seg_len, dtype=np.int32)
    group_id = position // GROUP
    crossed = group_id[:, None] ^ group_id[None, :]
    level_id = np.zeros((seg_len, seg_len), np.int32)
    for shift_bit in range(loc_bits):
        level_id = level_id + ((crossed >> shift_bit) > 0).astype(np.int32)
    causal = position[None, :] <= position[:, None]
    return [jnp.asarray(((level_id == level_num) & causal).astype(np.float32), jnp.float32) for level_num in range(loc_bits + 1)]


def segment_tables(n_bits):
    seg_ids = np.arange(N_SEQ)
    target = seg_ids[:, None]
    source = seg_ids[None, :]
    tables = []
    for level_bit in range(n_bits):
        member = (((target >> level_bit) & 1) == 1) & (((source >> level_bit) & 1) == 0) & ((target >> (level_bit + 1)) == (source >> (level_bit + 1)))
        tables.append(member.astype(np.float32))
    return jnp.asarray(np.stack(tables), jnp.float32)


def to_bf16(array):
    return lax.optimization_barrier(array.astype(jnp.bfloat16)).astype(jnp.float32)


def segment_pass(seg_query, seg_key, seg_value, seg_gain, seg_dout, far_stack, selects):
    seg_len = seg_query.shape[0]
    loc_bits = len(selects) - 1
    n_bits = far_stack.shape[0]
    score_scale = HD ** -0.5
    highest = lax.Precision.HIGHEST
    query_wide = seg_query.reshape(seg_len, H, HD).astype(jnp.float32)
    key_wide = seg_key.reshape(seg_len, H, HD).astype(jnp.float32)
    value_wide = seg_value.reshape(seg_len, H, HD).astype(jnp.float32)
    grad_wide = seg_dout.reshape(seg_len, H, HD).astype(jnp.float32)
    gains = seg_gain.reshape(seg_len, LEVELS, H)
    far_half = to_bf16(far_stack)
    scores = jnp.einsum('thd,shd->hts', query_wide, key_wide, precision=highest) * score_scale
    weight_mask = jnp.zeros((H, seg_len, seg_len), jnp.float32)
    for level_num in range(loc_bits + 1):
        weight_mask = weight_mask + selects[level_num][None] * gains[:, level_num, :].T[:, :, None]
    probs = to_bf16(scores * weight_mask)
    intra = jnp.einsum('hts,shd->thd', probs, value_wide, precision=highest)
    far_gain = jnp.transpose(gains[:, loc_bits + 1:loc_bits + 1 + n_bits, :], (1, 0, 2))
    projected = jnp.einsum('thd,bhde->bthe', query_wide, far_half, precision=highest) * score_scale
    cross = jnp.sum(far_gain[..., None] * projected, axis=0)
    attn = (intra + cross).reshape(seg_len, H * HD).astype(jnp.bfloat16)
    prob_grad = jnp.einsum('thd,shd->hts', grad_wide, value_wide, precision=highest)
    grad_v_in = jnp.einsum('hts,thd->shd', probs, grad_wide, precision=highest)
    energy = prob_grad * scores
    local_gain = jnp.stack([jnp.sum(energy * sel_mat[None], axis=2).T for sel_mat in selects], axis=1)
    score_grad = to_bf16(prob_grad * weight_mask)
    grad_q_in = jnp.einsum('hts,shd->thd', score_grad, key_wide, precision=highest) * score_scale
    grad_k_in = jnp.einsum('hts,thd->shd', score_grad, query_wide, precision=highest) * score_scale
    weighted = to_bf16(far_gain[..., None] * grad_wide[None])
    grad_q_far = jnp.einsum('bthe,bhde->thd', weighted, far_half, precision=highest) * score_scale
    cross_gain = jnp.transpose(jnp.sum(projected * grad_wide[None], axis=3), (1, 0, 2))
    weighted_query = to_bf16(far_gain[..., None] * query_wide[None])
    far_grad = jnp.einsum('bthd,the->bhde', weighted_query, grad_wide, precision=highest) * score_scale
    spare = LEVELS - loc_bits - 1 - n_bits
    gain_grad = jnp.concatenate([local_gain, cross_gain, jnp.zeros((seg_len, spare, H), jnp.float32)], axis=1)
    return attn, grad_q_in + grad_q_far, grad_k_in, grad_v_in, gain_grad.reshape(seg_len, LEVELS * H), far_grad


def reference(queries, keys, values, level_gain, out_weight, out_grad):
    highest = lax.Precision.HIGHEST
    n_bits = N_SEQ.bit_length() - 1
    selects = level_selects(TOK_DEV)
    tables = segment_tables(n_bits)
    attn_grad = jnp.dot(out_grad.reshape(BATCH * TOKENS, D), out_weight.T, preferred_element_type=jnp.float32).astype(jnp.bfloat16).reshape(BATCH, TOKENS, D)

    def batch_pass(items):
        seq_query, seq_key, seq_value, seq_gain, seq_dout = items
        seg_query = seq_query.reshape(N_SEQ, TOK_DEV, D)
        seg_key = seq_key.reshape(N_SEQ, TOK_DEV, D)
        seg_value = seq_value.reshape(N_SEQ, TOK_DEV, D)
        seg_gain = seq_gain.reshape(N_SEQ, TOK_DEV, LEVELS * H)
        seg_dout = seq_dout.reshape(N_SEQ, TOK_DEV, D)
        key_heads = seg_key.reshape(N_SEQ, TOK_DEV, H, HD).astype(jnp.float32)
        value_heads = seg_value.reshape(N_SEQ, TOK_DEV, H, HD).astype(jnp.float32)
        states = jnp.einsum('nthd,nthe->nhde', key_heads, value_heads, precision=highest)
        far_all = jnp.einsum('bnm,mhde->nbhde', tables, states, precision=highest)

        def one_segment(seg_items):
            return segment_pass(*seg_items, selects)

        attn, grad_q, grad_k_in, grad_v_in, gain_grad, far_grad = lax.map(one_segment, (seg_query, seg_key, seg_value, seg_gain, seg_dout, far_all))
        state_grad = jnp.einsum('bnm,nbhde->mhde', tables, far_grad, precision=highest)
        state_half = to_bf16(state_grad)
        grad_k = grad_k_in + jnp.einsum('nshe,nhde->nshd', value_heads, state_half, precision=highest)
        grad_v = grad_v_in + jnp.einsum('nshd,nhde->nshe', key_heads, state_half, precision=highest)
        return (attn.reshape(TOKENS, D), grad_q.reshape(TOKENS, D).astype(jnp.bfloat16), grad_k.reshape(TOKENS, D).astype(jnp.bfloat16), grad_v.reshape(TOKENS, D).astype(jnp.bfloat16), gain_grad.reshape(TOKENS, LEVELS * H))

    attn, query_grad, key_grad, value_grad, gain_grad = lax.map(batch_pass, (queries, keys, values, level_gain, attn_grad))
    weight_grad = lax.dot_general(attn.reshape(BATCH * TOKENS, D), out_grad.reshape(BATCH * TOKENS, D), (((0,), (0,)), ((), ())), preferred_element_type=jnp.float32)
    return query_grad, key_grad, value_grad, gain_grad, weight_grad
```

```python
import jax
import jax.numpy as jnp
from jax import lax
from jax.experimental import pallas as pl
from jax.experimental.pallas import tpu as pltpu
from jax.sharding import PartitionSpec as P

H = 16
HD = 128
T = 512
D = 2048
HALF = 1024
SCALE = HD**-0.5
BF = jnp.bfloat16
F32 = jnp.float32
MESH = pl.DeviceIdType.MESH
COLS = ((0, 384), (384, 384), (768, 256))
ORDERS = ((1, 2, 0), (2, 0, 1), (0, 1, 2))


def dot(a, b, ca, cb):
    return lax.dot_general(a, b, (((ca,), (cb,)), ((), ())), preferred_element_type=F32)


def rem(a, b):
    return lax.rem(a, jnp.int32(b))


def div(a, b):
    return lax.div(a, jnp.int32(b))


def flip(a):
    return a + 1 - 2 * rem(a, 2)


def recv_shapes():
    shapes = []
    for piece, (_, width) in enumerate(COLS):
        dims = [4, 4, 4]
        for axis in ORDERS[piece]:
            for left in (2, 1):
                dims[axis] = left
                shapes.append(tuple(dims) + (2, 16, width))
    return shapes


def kernel(
    q_in, k_in, v_in, gain_in, w_in, d_in,
    dq_out, dk_out, dv_out, gain_out, wg_out,
    q_v, k_v, v_v, d_v, gain_v, w_g, attn, dosib, wq, probs, g_v, far,
    st, st_send, st_sib, cs_send, r1, run_send, r2,
    gt, sg0, recv12, cs12, r1b, r2b, r3b, sgsum, tacc, wgout, finsend,
    acc0, acc1, acc2,
    *rest,
):
    recvs = [rest[0:6], rest[6:12], rest[12:18]]
    lsem, ssem, rsem, asem, arsem = rest[18:]
    accs = (acc0, acc1, acc2)
    seq = lax.axis_index("seq")
    bat = lax.axis_index("batch")
    core, z = rem(seq, 2), div(seq, 2)
    x, y = div(bat, 4), rem(bat, 4)
    sib = (z * 2 + 1 - core, bat)

    def load(i, src, dst):
        return pltpu.make_async_copy(src, dst, lsem.at[i])

    loads = [
        load(0, k_in.at[0], k_v),
        load(1, v_in.at[0], v_v),
        load(2, q_in.at[0], q_v),
        load(3, gain_in.at[0], gain_v),
        load(4, d_in.at[0], d_v),
    ]
    for c in loads:
        c.start()

    a1 = x * (1 - core) + y * core
    a2 = y * (1 - core) + x * core
    wloads, wsteps = [], []
    for p in (0, 1):
        b1, b2 = rem(a1 + p, 4), rem(a2 + p, 4)

        def dev(c1, c2, p=p):
            o1, o2 = rem(c1 + 4 - p, 4), rem(c2 + 4 - p, 4)
            return (seq, (o1 * 4 + o2) * (1 - core) + (o2 * 4 + o1) * core)

        own = w_in.at[pl.ds(pl.multiple_of(core * 64 + p * 32, 32), 32), :]
        wloads.append(load(5 + p, own, w_g.at[core, p, b1, b2]))
        pair1, pair2 = div(b1, 2) * 2, div(b2, 2) * 2
        base = 10 * p
        steps = []

        def add(src, dst, device, base=base, steps=steps):
            i = base + len(steps)
            steps.append(
                pltpu.make_async_remote_copy(
                    src_ref=src, dst_ref=dst, send_sem=ssem.at[i], recv_sem=rsem.at[i],
                    device_id=device, device_id_type=MESH,
                )
            )

        one = w_g.at[core, p, b1, b2]
        add(own, one, dev(flip(b1), b2))
        two = w_g.at[core, p, pl.ds(pair1, 2), b2]
        add(two, two, dev(3 - b1, b2))
        four = w_g.at[core, p, :, b2]
        add(four, four, dev(b1, flip(b2)))
        eight = w_g.at[core, p, :, pl.ds(pair2, 2)]
        add(eight, eight, dev(b1, 3 - b2))
        add(four, four, sib)
        four2 = w_g.at[core, p, :, flip(b2)]
        add(four2, four2, sib)
        eight2 = w_g.at[core, p, :, pl.ds(2 - pair2, 2)]
        add(eight2, eight2, sib)
        wsteps.append(steps)
    for c in wloads:
        c.start()

    barrier = pltpu.get_barrier_semaphore()
    neighbours = [
        sib,
        (seq, flip(x) * 4 + y), (seq, (3 - x) * 4 + y),
        (seq, x * 4 + flip(y)), (seq, x * 4 + 3 - y),
        (flip(z) * 2 + core, bat), ((3 - z) * 2 + core, bat),
    ]
    for n in neighbours:
        pl.semaphore_signal(barrier, inc=1, device_id=n, device_id_type=MESH)
    pl.semaphore_wait(barrier, len(neighbours))

    def remote(i, src, dst, device):
        return pltpu.make_async_remote_copy(
            src_ref=src, dst_ref=dst, send_sem=ssem.at[i], recv_sem=rsem.at[i],
            device_id=device, device_id_type=MESH,
        )

    sent = []

    def start(c):
        c.start()
        sent.append(c)

    for p in (0, 1):
        start(wsteps[p][0])

    dcopy = remote(
        20, d_in.at[0, :, pl.ds(pl.multiple_of((1 - core) * HALF, HALF), HALF)], dosib, sib
    )
    start(dcopy)

    zp1 = (flip(z) * 2 + core, bat)
    zp3 = ((3 - z) * 2 + core, bat)
    mine = pl.ds(core * 8, 8)
    theirs = pl.ds((1 - core) * 8, 8)
    e0 = remote(21, st_send, st_sib, sib)
    e1 = remote(22, cs_send, r1, zp1)
    e2 = remote(23, run_send, r2, zp3)
    f1 = far.at[mine, pl.ds(128, 128)]
    f2 = far.at[mine, pl.ds(256, 128)]
    e1s = remote(24, f1, f1, sib)
    e2s = remote(25, f2, f2, sib)
    c0 = remote(26, gt.at[0], sg0, sib)
    c12 = remote(27, gt.at[pl.ds(1, 2), theirs], recv12, sib)
    c1 = remote(28, cs12.at[0], r1b, zp1)
    c2 = remote(29, cs12.at[1], r2b, zp3)
    c3 = remote(30, r2b, r3b, zp1)
    c4 = remote(31, sgsum.at[mine], sgsum.at[mine], sib)
    bit = [rem(seq, 2).astype(F32), rem(z, 2).astype(F32), div(z, 2).astype(F32)]

    rot = [rem(z + core, 4), rem(x + core, 4), rem(y + core, 4)]

    def axis_dev(axis, r):
        o = rem(r + 4 - core, 4)
        if axis == 0:
            return (o * 2 + core, bat)
        if axis == 1:
            return (seq, o * 4 + y)
        return (seq, x * 4 + o)

    rs_copies, rs_keeps = [], []
    for piece in range(3):
        copies, keeps = [], []
        cur = [pl.ds(0, 4)] * 3
        for axis in ORDERS[piece]:
            a = rot[axis]
            for sub in (0, 1):
                give, keep = list(cur), list(cur)
                if sub == 0:
                    give[axis] = pl.ds(2 - 2 * div(a, 2), 2)
                    keep[axis] = pl.ds(2 * div(a, 2), 2)
                    to = axis_dev(axis, 3 - a)
                else:
                    give[axis] = pl.ds(flip(a), 1)
                    keep[axis] = pl.ds(a, 1)
                    to = axis_dev(axis, flip(a))
                n = len(copies)
                copies.append(
                    remote(32 + piece * 6 + n, accs[piece].at[tuple(give)], recvs[piece][n], to)
                )
                keeps.append(tuple(keep))
                cur = keep
        rs_copies.append(copies)
        rs_keeps.append(keeps)

    def rs_start(n):
        for piece in range(3):
            start(rs_copies[piece][n])

    def rs_add(n):
        for piece in range(3):
            rs_copies[piece][n].wait_recv()
            keep, recv, acc = rs_keeps[piece][n], recvs[piece][n], accs[piece]
            lead = keep[0]

            def body(i, _, keep=keep, recv=recv, acc=acc, lead=lead):
                at = (lead.start + i,) + keep[1:]
                acc[at] = (acc[at].astype(F32) + recv[i].astype(F32)).astype(BF)
                return 0

            lax.fori_loop(0, lead.size, body, 0)

    def hcols(h):
        return pl.ds(pl.multiple_of(h * HD, HD), HD)

    def rolled(h):
        return pltpu.roll(gain_v[...], rem(jnp.int32(HD) - h, HD), 1)

    loads[0].wait()
    loads[1].wait()

    def state_body(h, _):
        kh, vh = k_v[:, hcols(h)], v_v[:, hcols(h)]
        lo = dot(kh[:256], vh[:256], 0, 0)
        both = lo + dot(kh[256:], vh[256:], 0, 0)
        far[h, 384:512] = lo.astype(BF)
        st[h] = both
        st_send[h] = both.astype(BF)
        return 0

    lax.fori_loop(0, H, state_body, 0)
    start(e0)
    for p in (0, 1):
        wloads[p].wait()
        wsteps[p][0].wait_recv()
        start(wsteps[p][1])
    loads[2].wait()
    loads[3].wait()

    rr = lax.broadcasted_iota(jnp.int32, (128, 128), 0)
    cc = lax.broadcasted_iota(jnp.int32, (128, 128), 1)
    same = (rr < 64) == (cc < 64)
    m0 = (rr >= cc) & same
    m1 = (rr >= 64) & (cc < 64)

    def diag_mask(w0, w1):
        return jnp.where(m0, w0, jnp.where(m1, w1, 0.0))

    def ev_e0():
        e0.wait_recv()

        def body(h, _):
            far[h, 0:128] = (st_sib[h].astype(F32) * bit[0]).astype(BF)
            return 0

        lax.fori_loop(0, H, body, 0)

        def body2(i, _):
            total = st[core * 8 + i] + st_sib[core * 8 + i].astype(F32)
            st[core * 8 + i] = total
            cs_send[i] = total.astype(BF)
            return 0

        lax.fori_loop(0, 8, body2, 0)
        start(e1)

    def ev_e1():
        e1.wait_recv()

        def body(i, _):
            got = r1[i].astype(F32)
            far[core * 8 + i, 128:256] = (got * bit[1]).astype(BF)
            run_send[i] = (st[core * 8 + i] + got).astype(BF)
            return 0

        lax.fori_loop(0, 8, body, 0)
        start(e2)
        start(e1s)

    def ev_e2():
        e2.wait_recv()

        def body(i, _):
            far[core * 8 + i, 256:384] = (r2[i].astype(F32) * bit[2]).astype(BF)
            return 0

        lax.fori_loop(0, 8, body, 0)
        start(e2s)

    def ev_w2():
        for p in (0, 1):
            wsteps[p][1].wait_recv()
            start(wsteps[p][2])
            start(wsteps[p][4])

    def ev_w3():
        for p in (0, 1):
            wsteps[p][2].wait_recv()
            start(wsteps[p][3])
            start(wsteps[p][5])

    def ev_w4():
        for p in (0, 1):
            wsteps[p][3].wait_recv()
            start(wsteps[p][6])

    def probs_body(h, _):
        wr = rolled(h) * SCALE
        ws = [wr[:, 16 * l : 16 * l + 1] for l in range(7)]
        qh, kh = q_v[:, hcols(h)], k_v[:, hcols(h)]
        for blk in (0, 1):
            r0 = 256 * blk
            sc = dot(qh[r0 : r0 + 256], kh[r0 : r0 + 256], 1, 1)
            a, b = slice(r0, r0 + 128), slice(r0 + 128, r0 + 256)
            probs[h, blk, 0:128, 0:128] = (sc[:128, :128] * diag_mask(ws[0][a], ws[1][a])).astype(BF)
            probs[h, blk, 0:128, 128:256] = jnp.zeros((128, 128), BF)
            probs[h, blk, 128:256, 0:128] = (sc[128:, :128] * ws[2][b]).astype(BF)
            probs[h, blk, 128:256, 128:256] = (
                sc[128:, 128:] * diag_mask(ws[0][b], ws[1][b])
            ).astype(BF)
        qf = qh.astype(F32)
        for b in range(3):
            wq[h, :, 128 * b : 128 * b + 128] = (qf * ws[4 + b]).astype(BF)
        wq[h, 0:256, 384:512] = jnp.zeros((256, 128), BF)
        wq[h, 256:512, 384:512] = (qf[256:] * ws[3][256:]).astype(BF)
        return 0

    def run(body, cuts):
        at = 0
        for stop, event in cuts:
            if stop > at:
                lax.fori_loop(at, stop, body, 0)
            at = stop
            if event is not None:
                event()

    run(probs_body, [(3, ev_e0), (5, ev_w2), (11, ev_e1), (13, ev_w3), (16, None)])
    ev_e2()
    e1s.wait_recv()
    e2s.wait_recv()

    def attn_copy(h):
        return pltpu.make_async_remote_copy(
            src_ref=attn.at[0, h], dst_ref=attn.at[1, h], send_sem=asem.at[h],
            recv_sem=arsem.at[h], device_id=sib, device_id_type=MESH,
        )

    def attn_body(h, _):
        vh = v_v[:, hcols(h)]
        cross = dot(wq[h], far[h], 1, 0)
        for blk in (0, 1):
            r0 = 256 * blk
            out = dot(probs[h, blk], vh[r0 : r0 + 256], 1, 0) + cross[r0 : r0 + 256]
            attn[0, h, r0 : r0 + 256] = out.astype(BF)
        attn_copy(h).start()
        return 0

    lax.fori_loop(0, H, attn_body, 0)

    loads[4].wait()
    dcopy.wait_recv()

    def wg_body(h, _):
        attn_copy(h).wait_recv()
        own = d_v[:, pl.ds(pl.multiple_of(core * HALF, HALF), HALF)]
        part = dot(attn[0, h], own, 0, 0) + dot(attn[1, h], dosib[...], 0, 0)
        part = part.astype(BF)
        zd = rem(div(h, 4) + core, 4)
        cd = rem(div(h, 2), 2)
        for xi in (0, 1):
            xd = rem(2 * rem(h, 2) + xi + core, 4)
            for yi in range(4):
                yd = rem(yi + core, 4)
                row = (xi * 4 + yi) * 16
                for piece, (c0_, width) in enumerate(COLS):
                    accs[piece][zd, xd, yd, cd] = part[row : row + 16, c0_ : c0_ + width]
        return 0

    lax.fori_loop(0, H, wg_body, 0)
    rs_start(0)

    ev_w4()
    for p in (0, 1):
        for i in (4, 5, 6):
            wsteps[p][i].wait_recv()

    def g_body(i, _):
        blocks = []
        for j in (0, 1):
            h = 2 * i + j
            hx, hy = div(h, 4), rem(h, 4)
            hx1, hy1 = rem(hx + 1, 4), rem(hy + 1, 4)
            blocks += [w_g[0, 0, hx, hy], w_g[0, 1, hx1, hy1], w_g[1, 0, hy, hx], w_g[1, 1, hy1, hx1]]
        weight = jnp.concatenate(blocks, axis=0)
        out = dot(d_v[...], weight, 1, 1).astype(BF)
        for j in (0, 1):
            h = 2 * i + j
            gh = out[:, 128 * j : 128 * j + 128]
            g_v[h] = gh
            grads = dot(gh, wq[h], 0, 0)
            for b in range(3):
                gt[b, h] = (grads[:, 128 * b : 128 * b + 128] * bit[b]).astype(BF)
            gt[3, h] = grads[:, 384:512].astype(BF)
        return 0

    lax.fori_loop(0, H // 2, g_body, 0)
    start(c0)
    start(c12)

    def ev_c12():
        c12.wait_recv()

        def body(i, _):
            for b in (0, 1):
                cs12[b, i] = (gt[1 + b, core * 8 + i].astype(F32) + recv12[b, i].astype(F32)).astype(BF)
            return 0

        lax.fori_loop(0, 8, body, 0)
        start(c1)
        start(c2)

    def ev_c2():
        c2.wait_recv()
        start(c3)

    def ev_c3():
        c1.wait_recv()
        c3.wait_recv()

        def body(i, _):
            total = r1b[i].astype(F32) + r2b[i].astype(F32) + r3b[i].astype(F32)
            sgsum[core * 8 + i] = total.astype(BF)
            return 0

        lax.fori_loop(0, 8, body, 0)
        start(c4)

    def ev_rs(n):
        def event():
            rs_add(n)
            rs_start(n + 1)

        return event

    def wait_attn(h, _):
        attn_copy(h).wait_send()
        return 0

    lax.fori_loop(0, H, wait_attn, 0)
    tacc[...] = jnp.zeros_like(tacc)
    dsel = lax.broadcasted_iota(jnp.int32, (256, 128), 1) - 16 * div(
        lax.broadcasted_iota(jnp.int32, (256, 128), 0), 64
    )
    frow = lax.broadcasted_iota(jnp.int32, (512, 128), 0)
    dfar = lax.broadcasted_iota(jnp.int32, (512, 128), 1) - 64 - 16 * div(frow, 128)

    def dq_body(h, _):
        wr = rolled(h) * SCALE
        ws = [wr[:, 16 * l : 16 * l + 1] for l in range(7)]
        qf = q_v[:, hcols(h)].astype(F32)
        kh, vh, gh = k_v[:, hcols(h)], v_v[:, hcols(h)], g_v[h]
        sel = (dsel == h).astype(F32).astype(BF)
        fsel = (dfar == h).astype(F32).astype(BF)
        dq = None
        prods = []
        for b in range(3):
            pb = dot(gh, far[h, 128 * b : 128 * b + 128], 1, 1)
            prods.append((qf * pb).astype(BF))
            term = pb * ws[4 + b]
            dq = term if dq is None else dq + term
        p3 = dot(gh[256:], far[h, 384:512], 1, 1)
        prod3 = (qf[256:] * p3).astype(BF)
        p3 = p3 * ws[3][256:]
        for blk in (0, 1):
            r0 = 256 * blk
            pg = dot(gh[r0 : r0 + 256], vh[r0 : r0 + 256], 1, 1)
            a, b = slice(r0, r0 + 128), slice(r0 + 128, r0 + 256)
            top = jnp.concatenate(
                [(pg[:128, :128] * diag_mask(ws[0][a], ws[1][a])).astype(BF), jnp.zeros((128, 128), BF)], axis=1
            )
            bottom = jnp.concatenate(
                [
                    (pg[128:, :128] * ws[2][b]).astype(BF),
                    (pg[128:, 128:] * diag_mask(ws[0][b], ws[1][b])).astype(BF),
                ],
                axis=1,
            )
            sg = jnp.concatenate([top, bottom], axis=0)
            wq[h, r0 : r0 + 256, 0:256] = sg
            energy = (pg * probs[h, blk].astype(F32)).astype(BF)
            out = dot(sg, kh[r0 : r0 + 256], 1, 0) + dq[r0 : r0 + 256]
            fars = [prods[b][r0 : r0 + 256] for b in range(3)]
            if blk == 1:
                out = out + p3
                fars.append(prod3)
                sums = dot(jnp.concatenate(fars, axis=1), fsel, 1, 0)
            else:
                sums = dot(jnp.concatenate(fars, axis=1), fsel[:384], 1, 0)
            attn[0, h, r0 : r0 + 256] = out.astype(BF)
            tacc[r0 : r0 + 256] += sums + dot(energy, sel, 1, 0)
        pltpu.make_async_copy(attn.at[0, h], dq_out.at[0, :, hcols(h)], lsem.at[8 + h]).start()
        return 0

    run(
        dq_body,
        [(1, ev_c12), (6, ev_c2), (8, ev_rs(0)), (11, ev_rs(1)), (12, ev_c3), (14, ev_rs(2)), (15, ev_rs(3)), (16, None)],
    )
    c0.wait_recv()
    c4.wait_recv()

    def dk_body(h, _):
        base = sg0[h].astype(F32) + sgsum[h].astype(F32)
        halves = ((base + gt[3, h].astype(F32)).astype(BF), base.astype(BF))
        for blk in (0, 1):
            rows = pl.ds(256 * blk, 256)
            kb, vb, qb = k_v[rows, hcols(h)], v_v[rows, hcols(h)], q_v[rows, hcols(h)]
            gb = g_v[h, rows]
            dv = dot(probs[h, blk], gb, 0, 0) + dot(kb, halves[blk], 1, 1)
            dk = dot(wq[h, rows, 0:256], qb, 0, 0) + dot(vb, halves[blk], 1, 0)
            k_v[rows, hcols(h)] = dk.astype(BF)
            v_v[rows, hcols(h)] = dv.astype(BF)
        pltpu.make_async_copy(k_v.at[:, hcols(h)], dk_out.at[0, :, hcols(h)], lsem.at[24 + h]).start()
        pltpu.make_async_copy(v_v.at[:, hcols(h)], dv_out.at[0, :, hcols(h)], lsem.at[40 + h]).start()
        return 0

    run(dk_body, [(6, ev_rs(4)), (16, None)])

    lane = lax.broadcasted_iota(jnp.int32, (64, 128), 1)
    for i in range(8):
        rows = slice(64 * i, 64 * i + 64)
        g4 = i % 4
        t = tacc[rows]

        def moved(frm, to, t=t):
            shift = (to - frm) * 16 % 128
            return pltpu.roll(t, shift, 1) if shift else t

        res = jnp.where(lane < 16, moved(g4, 0), 0.0)
        if g4 % 2 == 1:
            res = jnp.where((lane >= 16) & (lane < 32), moved(g4 - 1, 1), res)
        if g4 >= 2:
            res = jnp.where((lane >= 32) & (lane < 48), moved(0, 2) + moved(1, 2), res)
        res = res / gain_v[rows]
        if i >= 4:
            res = jnp.where((lane >= 48) & (lane < 64), moved(7, 3) * SCALE, res)
        res = jnp.where((lane >= 64) & (lane < 112), t * SCALE, res)
        tacc[rows] = res
    gcopy = pltpu.make_async_copy(tacc, gain_out.at[0], lsem.at[56])
    gcopy.start()

    for piece, (c0_, width) in enumerate(COLS):
        rs_copies[piece][5].wait_recv()
        acc, recv = accs[piece], recvs[piece][5]
        own_at = (rot[0], rot[1], rot[2], core)
        sib_at = (rot[0], rot[1], rot[2], 1 - core)
        wgout[core, :, c0_ : c0_ + width] = acc[own_at].astype(F32) + recv[0, 0, 0, core].astype(F32)
        finsend[:, c0_ : c0_ + width] = acc[sib_at].astype(F32) + recv[0, 0, 0, 1 - core].astype(F32)
    last = remote(50, finsend, wgout.at[core], sib)
    start(last)
    last.wait_recv()
    outs = [
        pltpu.make_async_copy(wgout.at[i], wg_out.at[:, pl.ds(HALF * i, HALF)], lsem.at[57 + i])
        for i in (0, 1)
    ]
    for c in outs:
        c.start()
    for c in sent:
        c.wait_send()

    def wait_out(h, _):
        pltpu.make_async_copy(attn.at[0, h], dq_out.at[0, :, hcols(h)], lsem.at[8 + h]).wait()
        pltpu.make_async_copy(k_v.at[:, hcols(h)], dk_out.at[0, :, hcols(h)], lsem.at[24 + h]).wait()
        pltpu.make_async_copy(v_v.at[:, hcols(h)], dv_out.at[0, :, hcols(h)], lsem.at[40 + h]).wait()
        return 0

    lax.fori_loop(0, H, wait_out, 0)
    gcopy.wait()
    for c in outs:
        c.wait()


def local(queries, keys, values, level_gain, out_weight, out_grad):
    big = jax.ShapeDtypeStruct((1, T, D), BF)
    scratch = [
        pltpu.VMEM((T, D), BF),
        pltpu.VMEM((T, D), BF),
        pltpu.VMEM((T, D), BF),
        pltpu.VMEM((T, D), BF),
        pltpu.VMEM((T, HD), F32),
        pltpu.VMEM((2, 2, 4, 4, 32, D), BF),
        pltpu.VMEM((2, H, T, HD), BF),
        pltpu.VMEM((T, HALF), BF),
        pltpu.VMEM((H, T, T), BF),
        pltpu.VMEM((H, 2, 256, 256), BF),
        pltpu.VMEM((H, T, HD), BF),
        pltpu.VMEM((H, T, HD), BF),
        pltpu.VMEM((H, HD, HD), F32),
        pltpu.VMEM((H, HD, HD), BF),
        pltpu.VMEM((H, HD, HD), BF),
        pltpu.VMEM((8, HD, HD), BF),
        pltpu.VMEM((8, HD, HD), BF),
        pltpu.VMEM((8, HD, HD), BF),
        pltpu.VMEM((8, HD, HD), BF),
        pltpu.VMEM((4, H, HD, HD), BF),
        pltpu.VMEM((H, HD, HD), BF),
        pltpu.VMEM((2, 8, HD, HD), BF),
        pltpu.VMEM((2, 8, HD, HD), BF),
        pltpu.VMEM((8, HD, HD), BF),
        pltpu.VMEM((8, HD, HD), BF),
        pltpu.VMEM((8, HD, HD), BF),
        pltpu.VMEM((H, HD, HD), BF),
        pltpu.VMEM((T, HD), F32),
        pltpu.VMEM((2, 16, HALF), F32),
        pltpu.VMEM((16, HALF), F32),
    ]
    scratch += [pltpu.VMEM((4, 4, 4, 2, 16, width), BF) for _, width in COLS]
    scratch += [pltpu.VMEM(shape, BF) for shape in recv_shapes()]
    scratch += [
        pltpu.SemaphoreType.DMA((60,)),
        pltpu.SemaphoreType.DMA((52,)),
        pltpu.SemaphoreType.DMA((52,)),
        pltpu.SemaphoreType.DMA((H,)),
        pltpu.SemaphoreType.DMA((H,)),
    ]
    anyspace = pl.BlockSpec(memory_space=pl.ANY)
    return pl.pallas_call(
        kernel,
        out_shape=(
            big, big, big,
            jax.ShapeDtypeStruct((1, T, HD), F32),
            jax.ShapeDtypeStruct((16, D), F32),
        ),
        in_specs=[anyspace] * 6,
        out_specs=(anyspace,) * 5,
        scratch_shapes=scratch,
        compiler_params=pltpu.CompilerParams(
            collective_id=0, has_side_effects=True, vmem_limit_bytes=62 * 2**20
        ),
        cost_estimate=pl.CostEstimate(flops=20 * 10**9, bytes_accessed=16 * 2**20, transcendentals=0),
    )(queries, keys, values, level_gain, out_weight, out_grad)


def solution(mesh):
    tokens = P("batch", "seq", None)
    return jax.shard_map(
        local,
        mesh=mesh,
        in_specs=(tokens, tokens, tokens, tokens, P("batch", None), tokens),
        out_specs=(tokens, tokens, tokens, tokens, P(("seq", "batch"), None)),
        check_vma=False,
    )
```

```python
import jax
import jax.numpy as jnp
from jax import lax
from jax.experimental import pallas as pl
from jax.experimental.pallas import tpu as pltpu
from jax.sharding import PartitionSpec as P

H = 16
HD = 128
T = 512
D = 2048
HALF = 1024
SCALE = HD**-0.5
BF = jnp.bfloat16
F32 = jnp.float32
MESH = pl.DeviceIdType.MESH
COLS = ((0, 384), (384, 384), (768, 256))
ORDERS = ((1, 2, 0), (2, 0, 1), (0, 1, 2))


def dot(a, b, ca, cb):
    return lax.dot_general(a, b, (((ca,), (cb,)), ((), ())), preferred_element_type=F32)


def rem(a, b):
    return lax.rem(a, jnp.int32(b))


def div(a, b):
    return lax.div(a, jnp.int32(b))


def flip(a):
    return a + 1 - 2 * rem(a, 2)


def recv_shapes():
    shapes = []
    for piece, (_, width) in enumerate(COLS):
        dims = [4, 4, 4]
        for axis in ORDERS[piece]:
            for left in (2, 1):
                dims[axis] = left
                shapes.append(tuple(dims) + (2, 16, width))
    return shapes


def kernel(
    q_in, k_in, v_in, gain_in, w_in, d_in,
    dq_out, dk_out, dv_out, gain_out, wg_out,
    q_v, d_v, gain_v, w_g, attn_sib, dosib, wq, probs, g_v, far,
    st, st_sib, total, cs_send, r1, run_send, r2,
    gt, sg0, recv12, cs12, r1b, r2b, r3b, sgsum, wgout, finsend,
    acc0, acc1, acc2, fk0, fk1, fk2,
    *rest,
):
    recvs = [rest[0:6], rest[6:12], rest[12:18]]
    lsem, ssem, rsem, asem, arsem = rest[18:]
    accs = (acc0, acc1, acc2)
    kept = (fk0, fk1, fk2)
    k_v, v_v, own_v, tacc = dk_out.at[0], dv_out.at[0], dq_out.at[0], gain_out.at[0]
    seq = lax.axis_index("seq")
    bat = lax.axis_index("batch")
    core, z = rem(seq, 2), div(seq, 2)
    x, y = div(bat, 4), rem(bat, 4)
    sib = (z * 2 + 1 - core, bat)

    def load(i, src, dst):
        return pltpu.make_async_copy(src, dst, lsem.at[i])

    loads = [
        load(0, k_in.at[0], k_v),
        load(1, v_in.at[0], v_v),
        load(2, q_in.at[0], q_v),
        load(3, gain_in.at[0], gain_v),
        load(4, d_in.at[0], d_v),
    ]
    for c in loads:
        c.start()

    a1 = x * (1 - core) + y * core
    a2 = y * (1 - core) + x * core
    wloads, wsteps = [], []
    for p in (0, 1):
        b1, b2 = rem(a1 + p, 4), rem(a2 + p, 4)

        def dev(c1, c2, p=p):
            o1, o2 = rem(c1 + 4 - p, 4), rem(c2 + 4 - p, 4)
            return (seq, (o1 * 4 + o2) * (1 - core) + (o2 * 4 + o1) * core)

        own = w_in.at[pl.ds(pl.multiple_of(core * 64 + p * 32, 32), 32), :]
        wloads.append(load(5 + p, own, w_g.at[core, p, b1, b2]))
        pair1, pair2 = div(b1, 2) * 2, div(b2, 2) * 2
        base = 10 * p
        steps = []

        def add(src, dst, device, base=base, steps=steps):
            i = base + len(steps)
            steps.append(
                pltpu.make_async_remote_copy(
                    src_ref=src, dst_ref=dst, send_sem=ssem.at[i], recv_sem=rsem.at[i],
                    device_id=device, device_id_type=MESH,
                )
            )

        one = w_g.at[core, p, b1, b2]
        add(own, one, dev(flip(b1), b2))
        two = w_g.at[core, p, pl.ds(pair1, 2), b2]
        add(two, two, dev(3 - b1, b2))
        four = w_g.at[core, p, :, b2]
        add(four, four, dev(b1, flip(b2)))
        eight = w_g.at[core, p, :, pl.ds(pair2, 2)]
        add(eight, eight, dev(b1, 3 - b2))
        add(four, four, sib)
        four2 = w_g.at[core, p, :, flip(b2)]
        add(four2, four2, sib)
        eight2 = w_g.at[core, p, :, pl.ds(2 - pair2, 2)]
        add(eight2, eight2, sib)
        wsteps.append(steps)
    for c in wloads:
        c.start()

    barrier = pltpu.get_barrier_semaphore()
    neighbours = [
        sib,
        (seq, flip(x) * 4 + y), (seq, (3 - x) * 4 + y),
        (seq, x * 4 + flip(y)), (seq, x * 4 + 3 - y),
        (flip(z) * 2 + core, bat), ((3 - z) * 2 + core, bat),
    ]
    for n in neighbours:
        pl.semaphore_signal(barrier, inc=1, device_id=n, device_id_type=MESH)
    pl.semaphore_wait(barrier, len(neighbours))

    def remote(i, src, dst, device):
        return pltpu.make_async_remote_copy(
            src_ref=src, dst_ref=dst, send_sem=ssem.at[i], recv_sem=rsem.at[i],
            device_id=device, device_id_type=MESH,
        )

    sent = []

    def start(c):
        c.start()
        sent.append(c)

    for p in (0, 1):
        start(wsteps[p][0])

    dcopy = remote(
        20, d_in.at[0, :, pl.ds(pl.multiple_of((1 - core) * HALF, HALF), HALF)], dosib, sib
    )
    start(dcopy)

    zp1 = (flip(z) * 2 + core, bat)
    zp3 = ((3 - z) * 2 + core, bat)
    e0, e1, e2, es, c0, c12, c1, c2, c3, c4 = [[] for _ in range(10)]
    for j in (0, 1):
        four = pl.ds(4 * j, 4)
        n = 51 + 10 * j
        e0.append(remote(n, st.at[:, four], st_sib.at[:, four], sib))
        e1.append(remote(n + 1, cs_send.at[four], r1.at[four], zp1))
        e2.append(remote(n + 2, run_send.at[four], r2.at[four], zp3))
        fars = far.at[core, four, pl.ds(128, 256)]
        es.append(remote(n + 3, fars, fars, sib))
        c0.append(remote(n + 4, gt.at[0, :, four], sg0.at[:, four], sib))
        c12.append(remote(n + 5, gt.at[pl.ds(1, 2), 1 - core, four], recv12.at[:, four], sib))
        c1.append(remote(n + 6, cs12.at[0, four], r1b.at[four], zp1))
        c2.append(remote(n + 7, cs12.at[1, four], r2b.at[four], zp3))
        c3.append(remote(n + 8, r2b.at[four], r3b.at[four], zp1))
        sums = sgsum.at[core, four]
        c4.append(remote(n + 9, sums, sums, sib))
    bit = [rem(seq, 2).astype(F32), rem(z, 2).astype(F32), div(z, 2).astype(F32)]

    rot = [rem(z + core, 4), rem(x + core, 4), rem(y + core, 4)]

    def axis_dev(axis, r):
        o = rem(r + 4 - core, 4)
        if axis == 0:
            return (o * 2 + core, bat)
        if axis == 1:
            return (seq, o * 4 + y)
        return (seq, x * 4 + o)

    rs_copies, rs_keeps, rs_kept = [], [], []
    for piece in range(3):
        copies, keeps, local_keeps = [], [], []
        cur = [pl.ds(0, 4)] * 3
        cur_local = [pl.ds(0, 4)] * 3
        for axis in ORDERS[piece]:
            a = rot[axis]
            for sub in (0, 1):
                give, keep = list(cur), list(cur)
                if sub == 0:
                    give[axis] = pl.ds(2 - 2 * div(a, 2), 2)
                    keep[axis] = pl.ds(2 * div(a, 2), 2)
                    to = axis_dev(axis, 3 - a)
                else:
                    give[axis] = pl.ds(flip(a), 1)
                    keep[axis] = pl.ds(a, 1)
                    to = axis_dev(axis, flip(a))
                n = len(copies)
                copies.append(
                    remote(32 + piece * 6 + n, accs[piece].at[tuple(give)], recvs[piece][n], to)
                )
                keeps.append(tuple(keep))
                cur = keep
                if axis == ORDERS[piece][0]:
                    cur_local[axis] = pl.ds(0, 2) if sub == 0 else pl.ds(rem(a, 2), 1)
                else:
                    cur_local[axis] = keep[axis]
                local_keeps.append(tuple(cur_local))
        rs_copies.append(copies)
        rs_keeps.append(keeps)
        rs_kept.append(local_keeps)

    def rs_start(n):
        for piece in range(3):
            start(rs_copies[piece][n])

    def rs_add(n):
        for piece in range(3):
            rs_copies[piece][n].wait_recv()
            keep, local_keep = rs_keeps[piece][n], rs_kept[piece][n]
            recv, acc, f32s = recvs[piece][n], accs[piece], kept[piece]

            def body(i, _, keep=keep, local_keep=local_keep, recv=recv, acc=acc, f32s=f32s):
                at = (keep[0].start + i,) + keep[1:]
                local_at = (local_keep[0].start + i,) + local_keep[1:]
                before = acc[at].astype(F32) if n == 0 else f32s[local_at]
                value = before + recv[i].astype(F32)
                f32s[local_at] = value
                acc[at] = value.astype(BF)
                return 0

            lax.fori_loop(0, keep[0].size, body, 0)

    def hcols(h):
        return pl.ds(pl.multiple_of(h * HD, HD), HD)

    def rolled(h):
        return pltpu.roll(gain_v[...], rem(jnp.int32(HD) - h, HD), 1)

    loads[0].wait()
    loads[1].wait()

    def chunked(i):
        j, r = div(i, 8), rem(i, 8)
        return div(r, 4), 4 * j + rem(r, 4)

    def head(i):
        hi, lo = chunked(i)
        return hi * 8 + lo

    def state_body(i, _):
        hi, lo = chunked(i)
        h = hi * 8 + lo
        kh, vh = k_v[:, hcols(h)], v_v[:, hcols(h)]
        low = dot(kh[:256], vh[:256], 0, 0)
        far[hi, lo, 384:512] = low.astype(BF)
        st[hi, lo] = low + dot(kh[256:], vh[256:], 0, 0)
        return 0

    def ev_w1():
        for p in (0, 1):
            wloads[p].wait()
            wsteps[p][0].wait_recv()
            start(wsteps[p][1])

    def run(body, cuts):
        at = 0
        for stop, *events in cuts:
            if stop > at:
                lax.fori_loop(at, stop, body, 0)
            at = stop
            for event in events:
                event()

    def starts(*copies):
        def event():
            for c in copies:
                start(c)

        return event

    run(state_body, [(4, ev_w1), (8, starts(e0[0])), (16, starts(e0[1]))])
    loads[2].wait()
    loads[3].wait()

    rr = lax.broadcasted_iota(jnp.int32, (128, 128), 0)
    cc = lax.broadcasted_iota(jnp.int32, (128, 128), 1)
    same = (rr < 64) == (cc < 64)
    m0 = (rr >= cc) & same
    m1 = (rr >= 64) & (cc < 64)

    def diag_mask(w0, w1):
        return jnp.where(m0, w0, jnp.where(m1, w1, 0.0))

    def ev_e0(j):
        def event():
            e0[j].wait_recv()

            def body(i, _):
                m = 4 * j + i
                for hi in (0, 1):
                    far[hi, m, 0:128] = (st_sib[hi, m] * bit[0]).astype(BF)
                chip = st[core, m] + st_sib[core, m]
                total[m] = chip
                cs_send[m] = chip.astype(BF)
                return 0

            lax.fori_loop(0, 4, body, 0)
            start(e1[j])

        return event

    def ev_e1(j):
        def event():
            e1[j].wait_recv()

            def body(i, _):
                m = 4 * j + i
                got = r1[m].astype(F32)
                far[core, m, 128:256] = (got * bit[1]).astype(BF)
                run_send[m] = (total[m] + got).astype(BF)
                return 0

            lax.fori_loop(0, 4, body, 0)
            start(e2[j])

        return event

    def ev_e2(j):
        def event():
            e2[j].wait_recv()

            def body(i, _):
                m = 4 * j + i
                far[core, m, 256:384] = (r2[m].astype(F32) * bit[2]).astype(BF)
                return 0

            lax.fori_loop(0, 4, body, 0)
            start(es[j])

        return event

    def ev_es(j):
        return es[j].wait_recv

    def ev_w2():
        for p in (0, 1):
            wsteps[p][1].wait_recv()
            start(wsteps[p][2])
            start(wsteps[p][4])

    def ev_w3():
        for p in (0, 1):
            wsteps[p][2].wait_recv()
            start(wsteps[p][3])
            start(wsteps[p][5])

    def ev_w4():
        for p in (0, 1):
            wsteps[p][3].wait_recv()
            start(wsteps[p][6])

    def probs_body(h, _):
        wr = rolled(h)
        scaled = wr * SCALE
        ws = [(scaled if l < 3 else wr)[:, 16 * l : 16 * l + 1] for l in range(7)]
        qh, kh = q_v[:, hcols(h)], k_v[:, hcols(h)]
        for blk in (0, 1):
            r0 = 256 * blk
            sc = dot(qh[r0 : r0 + 256], kh[r0 : r0 + 256], 1, 1)
            a, b = slice(r0, r0 + 128), slice(r0 + 128, r0 + 256)
            probs[h, blk, 0:128, 0:128] = (sc[:128, :128] * diag_mask(ws[0][a], ws[1][a])).astype(BF)
            probs[h, blk, 0:128, 128:256] = jnp.zeros((128, 128), BF)
            probs[h, blk, 128:256, 0:128] = (sc[128:, :128] * ws[2][b]).astype(BF)
            probs[h, blk, 128:256, 128:256] = (
                sc[128:, 128:] * diag_mask(ws[0][b], ws[1][b])
            ).astype(BF)
        qf = qh.astype(F32)
        for b in range(3):
            wq[h, :, 128 * b : 128 * b + 128] = (qf * ws[4 + b]).astype(BF)
        wq[h, 0:256, 384:512] = jnp.zeros((256, 128), BF)
        wq[h, 256:512, 384:512] = (qf[256:] * ws[3][256:]).astype(BF)
        return 0

    run(
        probs_body,
        [
            (1, ev_e0(0)), (2, ev_w2), (3, ev_e0(1)), (7, ev_e1(0)), (11, ev_e1(1)),
            (14, ev_e2(0)), (15, ev_w3), (16, ev_es(0)),
        ],
    )

    def attn_copy(h):
        return pltpu.make_async_remote_copy(
            src_ref=own_v.at[:, hcols(h)], dst_ref=attn_sib.at[h], send_sem=asem.at[h],
            recv_sem=arsem.at[h], device_id=sib, device_id_type=MESH,
        )

    def attn_body(i, _):
        hi, lo = chunked(i)
        h = hi * 8 + lo
        vh = v_v[:, hcols(h)]
        cross = dot(wq[h], far[hi, lo], 1, 0) * SCALE
        for blk in (0, 1):
            r0 = 256 * blk
            out = dot(probs[h, blk], vh[r0 : r0 + 256], 1, 0) + cross[r0 : r0 + 256]
            own_v[r0 : r0 + 256, hcols(h)] = out.astype(BF)
        attn_copy(h).start()
        return 0

    run(attn_body, [(4, ev_e2(1)), (8, ev_es(1)), (16,)])

    loads[4].wait()
    dcopy.wait_recv()

    def wg_body(i, _):
        h = head(i)
        attn_copy(h).wait_recv()
        own = d_v[:, pl.ds(pl.multiple_of(core * HALF, HALF), HALF)]
        part = dot(own_v[:, hcols(h)], own, 0, 0) + dot(attn_sib[h], dosib[...], 0, 0)
        part = part.astype(BF)
        zd = rem(div(h, 4) + core, 4)
        cd = rem(div(h, 2), 2)
        for xi in (0, 1):
            xd = rem(2 * rem(h, 2) + xi + core, 4)
            for yi in range(4):
                yd = rem(yi + core, 4)
                row = (xi * 4 + yi) * 16
                for piece, (c0_, width) in enumerate(COLS):
                    accs[piece][zd, xd, yd, cd] = part[row : row + 16, c0_ : c0_ + width]
        return 0

    run(wg_body, [(10, ev_w4), (16,)])
    rs_start(0)

    for p in (0, 1):
        for i in (4, 5, 6):
            wsteps[p][i].wait_recv()

    def g_body(i, _):
        blocks = []
        hi, lo = chunked(2 * i)
        for j in (0, 1):
            h = hi * 8 + lo + j
            hx, hy = div(h, 4), rem(h, 4)
            hx1, hy1 = rem(hx + 1, 4), rem(hy + 1, 4)
            blocks += [w_g[0, 0, hx, hy], w_g[0, 1, hx1, hy1], w_g[1, 0, hy, hx], w_g[1, 1, hy1, hx1]]
        weight = jnp.concatenate(blocks, axis=0)
        out = dot(d_v[...], weight, 1, 1).astype(BF)
        for j in (0, 1):
            h = hi * 8 + lo + j
            gh = out[:, 128 * j : 128 * j + 128]
            g_v[h] = gh
            grads = dot(gh, wq[h], 0, 0)
            for b in range(3):
                gt[b, hi, lo + j] = (grads[:, 128 * b : 128 * b + 128] * (bit[b] * SCALE)).astype(BF)
            gt[3, hi, lo + j] = (grads[:, 384:512] * SCALE).astype(BF)
        return 0

    def ev_c12(j):
        def event():
            c12[j].wait_recv()

            def body(i, _):
                m = 4 * j + i
                for b in (0, 1):
                    both = gt[1 + b, core, m].astype(F32) + recv12[b, m].astype(F32)
                    cs12[b, m] = both.astype(BF)
                return 0

            lax.fori_loop(0, 4, body, 0)
            start(c1[j])
            start(c2[j])

        return event

    def ev_c2(j):
        def event():
            c2[j].wait_recv()
            start(c3[j])

        return event

    def ev_c3(j):
        def event():
            c1[j].wait_recv()
            c3[j].wait_recv()

            def body(i, _):
                m = 4 * j + i
                both = r1b[m].astype(F32) + r2b[m].astype(F32) + r3b[m].astype(F32)
                sgsum[core, m] = both.astype(BF)
                return 0

            lax.fori_loop(0, 4, body, 0)
            start(c4[j])

        return event

    run(
        g_body,
        [(4, starts(c0[0], c12[0])), (5, ev_c12(0)), (8, starts(c0[1], c12[1]))],
    )

    def ev_rs(n):
        def event():
            rs_add(n)
            rs_start(n + 1)

        return event

    def wait_attn(h, _):
        attn_copy(h).wait_send()
        return 0

    lax.fori_loop(0, H, wait_attn, 0)
    tacc[...] = jnp.zeros_like(tacc)
    dsel = lax.broadcasted_iota(jnp.int32, (256, 128), 1) - 16 * div(
        lax.broadcasted_iota(jnp.int32, (256, 128), 0), 64
    )
    frow = lax.broadcasted_iota(jnp.int32, (512, 128), 0)
    dfar = lax.broadcasted_iota(jnp.int32, (512, 128), 1) - 64 - 16 * div(frow, 128)

    def dq_body(h, _):
        wr = rolled(h)
        ws = [wr[:, 16 * l : 16 * l + 1] for l in range(7)]
        qf = q_v[:, hcols(h)].astype(F32)
        kh, vh, gh = k_v[:, hcols(h)], v_v[:, hcols(h)], g_v[h]
        fh = far.at[div(h, 8), rem(h, 8)]
        sel = (dsel == h).astype(F32).astype(BF)
        fsel = (dfar == h).astype(F32).astype(BF)
        dq = None
        prods = []
        for b in range(3):
            pb = dot(gh, fh[128 * b : 128 * b + 128], 1, 1)
            prods.append((qf * pb).astype(BF))
            term = pb * ws[4 + b]
            dq = term if dq is None else dq + term
        p3 = dot(gh[256:], fh[384:512], 1, 1)
        prod3 = (qf[256:] * p3).astype(BF)
        p3 = p3 * ws[3][256:]
        for blk in (0, 1):
            r0 = 256 * blk
            pg = dot(gh[r0 : r0 + 256], vh[r0 : r0 + 256], 1, 1)
            a, b = slice(r0, r0 + 128), slice(r0 + 128, r0 + 256)
            top = jnp.concatenate(
                [(pg[:128, :128] * diag_mask(ws[0][a], ws[1][a])).astype(BF), jnp.zeros((128, 128), BF)], axis=1
            )
            bottom = jnp.concatenate(
                [
                    (pg[128:, :128] * ws[2][b]).astype(BF),
                    (pg[128:, 128:] * diag_mask(ws[0][b], ws[1][b])).astype(BF),
                ],
                axis=1,
            )
            sg = jnp.concatenate([top, bottom], axis=0)
            wq[h, r0 : r0 + 256, 0:256] = sg
            energy = (pg * probs[h, blk].astype(F32)).astype(BF)
            out = dot(sg, kh[r0 : r0 + 256], 1, 0) + dq[r0 : r0 + 256]
            fars = [prods[b][r0 : r0 + 256] for b in range(3)]
            if blk == 1:
                out = out + p3
                fars.append(prod3)
                sums = dot(jnp.concatenate(fars, axis=1), fsel, 1, 0)
            else:
                sums = dot(jnp.concatenate(fars, axis=1), fsel[:384], 1, 0)
            own_v[r0 : r0 + 256, hcols(h)] = (out * SCALE).astype(BF)
            tacc[r0 : r0 + 256] += sums + dot(energy, sel, 1, 0)
        return 0

    run(
        dq_body,
        [
            (1, ev_rs(0), ev_c12(1)), (3, ev_c2(0)), (6, ev_rs(1)), (7, ev_c2(1)), (8, ev_c3(0)),
            (10, ev_rs(2)), (12, ev_rs(3), ev_c3(1)), (14, ev_rs(4)), (16,),
        ],
    )
    for j in (0, 1):
        c0[j].wait_recv()
        c4[j].wait_recv()

    def dk_body(h, _):
        hi, lo = div(h, 8), rem(h, 8)
        base = sg0[hi, lo].astype(F32) + sgsum[hi, lo].astype(F32)
        halves = ((base + gt[3, hi, lo].astype(F32)).astype(BF), base.astype(BF))
        for blk in (0, 1):
            rows = pl.ds(256 * blk, 256)
            kb, vb, qb = k_v[rows, hcols(h)], v_v[rows, hcols(h)], q_v[rows, hcols(h)]
            gb = g_v[h, rows]
            dv = dot(probs[h, blk], gb, 0, 0) + dot(kb, halves[blk], 1, 1)
            dk = dot(wq[h, rows, 0:256], qb, 0, 0) * SCALE + dot(vb, halves[blk], 1, 0)
            k_v[rows, hcols(h)] = dk.astype(BF)
            v_v[rows, hcols(h)] = dv.astype(BF)
        return 0

    def finish():
        for piece, (first, width) in enumerate(COLS):
            rs_copies[piece][5].wait_recv()
            f32s, recv = kept[piece], recvs[piece][5]
            at = tuple(s.start for s in rs_kept[piece][5])
            cols = slice(first, first + width)
            wgout[core, :, cols] = f32s[at + (core,)] + recv[0, 0, 0, core].astype(F32)
            finsend[:, cols] = f32s[at + (1 - core,)] + recv[0, 0, 0, 1 - core].astype(F32)
        start(last)

    last = remote(50, finsend, wgout.at[core], sib)
    run(dk_body, [(6, finish), (16,)])

    lane = lax.broadcasted_iota(jnp.int32, (64, 128), 1)
    for i in range(8):
        rows = slice(64 * i, 64 * i + 64)
        g4 = i % 4
        t = tacc[rows]

        def moved(frm, to, t=t):
            shift = (to - frm) * 16 % 128
            return pltpu.roll(t, shift, 1) if shift else t

        res = jnp.where(lane < 16, moved(g4, 0), 0.0)
        if g4 % 2 == 1:
            res = jnp.where((lane >= 16) & (lane < 32), moved(g4 - 1, 1), res)
        if g4 >= 2:
            res = jnp.where((lane >= 32) & (lane < 48), moved(0, 2) + moved(1, 2), res)
        res = res / gain_v[rows]
        if i >= 4:
            res = jnp.where((lane >= 48) & (lane < 64), moved(7, 3) * SCALE, res)
        res = jnp.where((lane >= 64) & (lane < 112), t * SCALE, res)
        tacc[rows] = res
    last.wait_recv()
    for i in (0, 1):
        wg_out[:, HALF * i : HALF * i + HALF] = wgout[i]
    for c in sent:
        c.wait_send()


def local(queries, keys, values, level_gain, out_weight, out_grad):
    big = pltpu.VMEM((1, T, D), BF)
    state = (2, 8, HD, HD)
    scratch = [
        pltpu.VMEM((T, D), BF),
        pltpu.VMEM((T, D), BF),
        pltpu.VMEM((T, HD), F32),
        pltpu.VMEM((2, 2, 4, 4, 32, D), BF),
        pltpu.VMEM((H, T, HD), BF),
        pltpu.VMEM((T, HALF), BF),
        pltpu.VMEM((H, T, T), BF),
        pltpu.VMEM((H, 2, 256, 256), BF),
        pltpu.VMEM((H, T, HD), BF),
        pltpu.VMEM((2, 8, T, HD), BF),
        pltpu.VMEM(state, F32),
        pltpu.VMEM(state, F32),
        pltpu.VMEM((8, HD, HD), F32),
        pltpu.VMEM((8, HD, HD), BF),
        pltpu.VMEM((8, HD, HD), BF),
        pltpu.VMEM((8, HD, HD), BF),
        pltpu.VMEM((8, HD, HD), BF),
        pltpu.VMEM((4,) + state, BF),
        pltpu.VMEM(state, BF),
        pltpu.VMEM(state, BF),
        pltpu.VMEM(state, BF),
        pltpu.VMEM((8, HD, HD), BF),
        pltpu.VMEM((8, HD, HD), BF),
        pltpu.VMEM((8, HD, HD), BF),
        pltpu.VMEM(state, BF),
        pltpu.VMEM((2, 16, HALF), F32),
        pltpu.VMEM((16, HALF), F32),
    ]
    scratch += [pltpu.VMEM((4, 4, 4, 2, 16, width), BF) for _, width in COLS]
    scratch += [pltpu.VMEM(shape, F32) for shape in recv_shapes()[::6]]
    scratch += [pltpu.VMEM(shape, BF) for shape in recv_shapes()]
    scratch += [
        pltpu.SemaphoreType.DMA((8,)),
        pltpu.SemaphoreType.DMA((72,)),
        pltpu.SemaphoreType.DMA((72,)),
        pltpu.SemaphoreType.DMA((H,)),
        pltpu.SemaphoreType.DMA((H,)),
    ]
    anyspace = pl.BlockSpec(memory_space=pl.ANY)
    return pl.pallas_call(
        kernel,
        out_shape=(
            big, big, big,
            pltpu.VMEM((1, T, HD), F32),
            pltpu.VMEM((16, D), F32),
        ),
        in_specs=[anyspace] * 6,
        out_specs=(pl.BlockSpec(memory_space=pltpu.VMEM),) * 5,
        scratch_shapes=scratch,
        compiler_params=pltpu.CompilerParams(
            collective_id=0, has_side_effects=True, vmem_limit_bytes=57 * 2**20
        ),
        cost_estimate=pl.CostEstimate(flops=20 * 10**9, bytes_accessed=16 * 2**20, transcendentals=0),
    )(queries, keys, values, level_gain, out_weight, out_grad)


def solution(mesh):
    tokens = P("batch", "seq", None)
    return jax.shard_map(
        local,
        mesh=mesh,
        in_specs=(tokens, tokens, tokens, tokens, P("batch", None), tokens),
        out_specs=(tokens, tokens, tokens, tokens, P(("seq", "batch"), None)),
        check_vma=False,
    )
```

```python
import jax
import jax.numpy as jnp
from jax import lax
from jax.experimental import pallas as pl
from jax.experimental.pallas import tpu as pltpu
from jax.sharding import PartitionSpec as P

H = 16
HD = 128
T = 512
D = 2048
HALF = 1024
SCALE = HD**-0.5
BF = jnp.bfloat16
F32 = jnp.float32
MESH = pl.DeviceIdType.MESH
COLS = ((0, 384), (384, 384), (768, 256))
ORDERS = ((1, 2, 0), (2, 0, 1), (0, 1, 2))


def dot(a, b, ca, cb):
    return lax.dot_general(a, b, (((ca,), (cb,)), ((), ())), preferred_element_type=F32)


def rem(a, b):
    return lax.rem(a, jnp.int32(b))


def div(a, b):
    return lax.div(a, jnp.int32(b))


def flip(a):
    return a + 1 - 2 * rem(a, 2)


def recv_shapes():
    shapes = []
    for piece, (_, width) in enumerate(COLS):
        dims = [4, 4, 4]
        for axis in ORDERS[piece]:
            for left in (2, 1):
                dims[axis] = left
                shapes.append(tuple(dims) + (2, 16, width))
    return shapes


def kernel(
    q_in, k_in, v_in, gain_in, w_in, d_in,
    dq_out, dk_out, dv_out, gain_out, wg_out,
    q_v, d_v, gain_v, w_g, attn_sib, dosib, wq, probs, g_v, far,
    st, st_sib, cs_send, r1, r2, r3,
    gt, sg0, recv12, cs12, r1b, r2b, r3b, sgsum, wgout, finsend,
    acc0, acc1, acc2, fk0, fk1, fk2,
    *rest,
):
    recvs = [rest[0:6], rest[6:12], rest[12:18]]
    lsem, ssem, rsem, asem, arsem = rest[18:]
    accs = (acc0, acc1, acc2)
    kept = (fk0, fk1, fk2)
    k_v, v_v, own_v, tacc = dk_out.at[0], dv_out.at[0], dq_out.at[0], gain_out.at[0]
    seq = lax.axis_index("seq")
    bat = lax.axis_index("batch")
    core, z = rem(seq, 2), div(seq, 2)
    x, y = div(bat, 4), rem(bat, 4)
    sib = (z * 2 + 1 - core, bat)

    def load(i, src, dst):
        return pltpu.make_async_copy(src, dst, lsem.at[i])

    loads = [
        load(0, k_in.at[0], k_v),
        load(1, v_in.at[0], v_v),
        load(2, q_in.at[0], q_v),
        load(3, gain_in.at[0], gain_v),
        load(4, d_in.at[0], d_v),
    ]
    for c in loads:
        c.start()

    a1 = x * (1 - core) + y * core
    a2 = y * (1 - core) + x * core
    wloads, wsteps = [], []
    for p in (0, 1):
        b1, b2 = rem(a1 + p, 4), rem(a2 + p, 4)

        def dev(c1, c2, p=p):
            o1, o2 = rem(c1 + 4 - p, 4), rem(c2 + 4 - p, 4)
            return (seq, (o1 * 4 + o2) * (1 - core) + (o2 * 4 + o1) * core)

        own32 = w_in.at[pl.ds(pl.multiple_of(core * 64 + p * 32, 32), 32), :]
        wloads.append(load(5 + p, own32, w_g.at[core, p, b1, b2]))
        pair1, pair2 = div(b1, 2) * 2, div(b2, 2) * 2
        for k in (0, 1):
            sub = pl.ds(16 * k, 16)
            own = w_in.at[pl.ds(pl.multiple_of(core * 64 + p * 32 + k * 16, 16), 16), :]
            steps = []

            def add(src, dst, device, base=80 + (p * 2 + k) * 7, steps=steps):
                i = base + len(steps)
                steps.append(
                    pltpu.make_async_remote_copy(
                        src_ref=src, dst_ref=dst, send_sem=ssem.at[i], recv_sem=rsem.at[i],
                        device_id=device, device_id_type=MESH,
                    )
                )

            add(own, w_g.at[core, p, b1, b2, sub], dev(flip(b1), b2))
            two = w_g.at[core, p, pl.ds(pair1, 2), b2, sub]
            add(two, two, dev(3 - b1, b2))
            four = w_g.at[core, p, :, b2, sub]
            add(four, four, dev(b1, flip(b2)))
            eight = w_g.at[core, p, :, pl.ds(pair2, 2), sub]
            add(eight, eight, dev(b1, 3 - b2))
            add(four, four, sib)
            four2 = w_g.at[core, p, :, flip(b2), sub]
            add(four2, four2, sib)
            eight2 = w_g.at[core, p, :, pl.ds(2 - pair2, 2), sub]
            add(eight2, eight2, sib)
            wsteps.append(steps)
    for c in wloads:
        c.start()

    barrier = pltpu.get_barrier_semaphore()
    neighbours = [
        sib,
        (seq, flip(x) * 4 + y), (seq, (3 - x) * 4 + y),
        (seq, x * 4 + flip(y)), (seq, x * 4 + 3 - y),
        (flip(z) * 2 + core, bat), ((3 - z) * 2 + core, bat), (rem(z + 2, 4) * 2 + core, bat),
    ]
    for n in neighbours:
        pl.semaphore_signal(barrier, inc=1, device_id=n, device_id_type=MESH)
    pl.semaphore_wait(barrier, len(neighbours))

    def remote(i, src, dst, device):
        return pltpu.make_async_remote_copy(
            src_ref=src, dst_ref=dst, send_sem=ssem.at[i], recv_sem=rsem.at[i],
            device_id=device, device_id_type=MESH,
        )

    sent = []

    def start(c):
        c.start()
        sent.append(c)

    for k in (0, 1):
        for p in (0, 1):
            start(wsteps[2 * p + k][0])

    dcopy = remote(
        20, d_in.at[0, :, pl.ds(pl.multiple_of((1 - core) * HALF, HALF), HALF)], dosib, sib
    )
    start(dcopy)

    zp1 = (flip(z) * 2 + core, bat)
    zp3 = ((3 - z) * 2 + core, bat)
    zp2 = (rem(z + 2, 4) * 2 + core, bat)
    e0, e1, e2, e3, es, c0, c12, c1, c2, c3, c4 = [[] for _ in range(11)]
    for j in (0, 1):
        four = pl.ds(4 * j, 4)
        n = 51 + 11 * j
        e0.append(remote(n, st.at[:, four], st_sib.at[:, four], sib))
        e1.append(remote(n + 1, cs_send.at[four], r1.at[four], zp1))
        e2.append(remote(n + 2, cs_send.at[four], r2.at[four], zp3))
        e3.append(remote(n + 10, cs_send.at[four], r3.at[four], zp2))
        fars = far.at[core, four, pl.ds(128, 256)]
        es.append(remote(n + 3, fars, fars, sib))
        c0.append(remote(n + 4, gt.at[0, :, four], sg0.at[:, four], sib))
        c12.append(remote(n + 5, gt.at[pl.ds(1, 2), 1 - core, four], recv12.at[:, four], sib))
        c1.append(remote(n + 6, cs12.at[0, four], r1b.at[four], zp1))
        c2.append(remote(n + 7, cs12.at[1, four], r2b.at[four], zp3))
        c3.append(remote(n + 8, cs12.at[1, four], r3b.at[four], zp2))
        sums = sgsum.at[core, four]
        c4.append(remote(n + 9, sums, sums, sib))
    bit = [rem(seq, 2).astype(F32), rem(z, 2).astype(F32), div(z, 2).astype(F32)]

    rot = [rem(z + core, 4), rem(x + core, 4), rem(y + core, 4)]

    def axis_dev(axis, r):
        o = rem(r + 4 - core, 4)
        if axis == 0:
            return (o * 2 + core, bat)
        if axis == 1:
            return (seq, o * 4 + y)
        return (seq, x * 4 + o)

    rs_copies, rs_keeps, rs_kept = [], [], []
    for piece in range(3):
        copies, keeps, local_keeps = [], [], []
        cur = [pl.ds(0, 4)] * 3
        cur_local = [pl.ds(0, 4)] * 3
        for axis in ORDERS[piece]:
            a = rot[axis]
            for sub in (0, 1):
                give, keep = list(cur), list(cur)
                if sub == 0:
                    give[axis] = pl.ds(2 - 2 * div(a, 2), 2)
                    keep[axis] = pl.ds(2 * div(a, 2), 2)
                    to = axis_dev(axis, 3 - a)
                else:
                    give[axis] = pl.ds(flip(a), 1)
                    keep[axis] = pl.ds(a, 1)
                    to = axis_dev(axis, flip(a))
                n = len(copies)
                copies.append(
                    remote(32 + piece * 6 + n, accs[piece].at[tuple(give)], recvs[piece][n], to)
                )
                keeps.append(tuple(keep))
                cur = keep
                if axis == ORDERS[piece][0]:
                    cur_local[axis] = pl.ds(0, 2) if sub == 0 else pl.ds(rem(a, 2), 1)
                else:
                    cur_local[axis] = keep[axis]
                local_keeps.append(tuple(cur_local))
        rs_copies.append(copies)
        rs_keeps.append(keeps)
        rs_kept.append(local_keeps)

    def rs_start(n):
        for piece in range(3):
            start(rs_copies[piece][n])

    def rs_add(n):
        for piece in range(3):
            rs_copies[piece][n].wait_recv()
            keep, local_keep = rs_keeps[piece][n], rs_kept[piece][n]
            recv, acc, f32s = recvs[piece][n], accs[piece], kept[piece]

            def body(i, _, keep=keep, local_keep=local_keep, recv=recv, acc=acc, f32s=f32s):
                at = (keep[0].start + i,) + keep[1:]
                local_at = (local_keep[0].start + i,) + local_keep[1:]
                before = acc[at].astype(F32) if n == 0 else f32s[local_at]
                value = before + recv[i].astype(F32)
                f32s[local_at] = value
                acc[at] = value.astype(BF)
                return 0

            lax.fori_loop(0, keep[0].size, body, 0)

    def hcols(h):
        return pl.ds(pl.multiple_of(h * HD, HD), HD)

    def rolled(h):
        return pltpu.roll(gain_v[...], rem(jnp.int32(HD) - h, HD), 1)

    loads[0].wait()
    loads[1].wait()

    def chunked(i):
        j, r = div(i, 8), rem(i, 8)
        return div(r, 4), 4 * j + rem(r, 4)

    def head(i):
        hi, lo = chunked(i)
        return hi * 8 + lo

    def state_body(i, _):
        hi, lo = chunked(i)
        h = hi * 8 + lo
        kh, vh = k_v[:, hcols(h)], v_v[:, hcols(h)]
        low = dot(kh[:256], vh[:256], 0, 0)
        far[hi, lo, 384:512] = low.astype(BF)
        st[hi, lo] = low + dot(kh[256:], vh[256:], 0, 0)
        return 0

    def ev_w(n, k):
        def event():
            for p in (0, 1):
                steps = wsteps[2 * p + k]
                if n == 1 and k == 0:
                    wloads[p].wait()
                steps[n - 1].wait_recv()
                if n < 4:
                    start(steps[n])
                if n > 1:
                    start(steps[n + 2])

        return event

    def run(body, cuts, count=H, step=1):
        def stepped(i, _):
            for at, *events in cuts:
                if at < count:

                    @pl.when(i * step == at)
                    def _():
                        for event in events:
                            event()

            for j in range(step):
                body(i * step + j, 0)
            return 0

        lax.fori_loop(0, count // step, stepped, 0)
        for at, *events in cuts:
            if at >= count:
                for event in events:
                    event()

    def starts(*copies):
        def event():
            for c in copies:
                start(c)

        return event

    run(
        state_body,
        [(4, ev_w(1, 0)), (8, starts(e0[0]), ev_w(1, 1)), (16, starts(e0[1]))],
        step=2,
    )
    loads[2].wait()
    loads[3].wait()

    rr = lax.broadcasted_iota(jnp.int32, (128, 128), 0)
    cc = lax.broadcasted_iota(jnp.int32, (128, 128), 1)
    same = (rr < 64) == (cc < 64)
    m0 = (rr >= cc) & same
    m1 = (rr >= 64) & (cc < 64)

    def diag_mask(w0, w1):
        return jnp.where(m0, w0, jnp.where(m1, w1, 0.0))

    def ev_e0(j):
        def event():
            e0[j].wait_recv()

            def body(i, _):
                m = 4 * j + i
                for hi in (0, 1):
                    far[hi, m, 0:128] = (st_sib[hi, m] * bit[0]).astype(BF)
                cs_send[m] = (st[core, m] + st_sib[core, m]).astype(BF)
                return 0

            lax.fori_loop(0, 4, body, 0)
            start(e1[j])
            start(e2[j])
            start(e3[j])

        return event

    def ev_e1(j):
        def event():
            e1[j].wait_recv()
            e2[j].wait_recv()
            e3[j].wait_recv()

            def body(i, _):
                m = 4 * j + i
                far[core, m, 128:256] = (r1[m].astype(F32) * bit[1]).astype(BF)
                far[core, m, 256:384] = ((r2[m].astype(F32) + r3[m].astype(F32)) * bit[2]).astype(BF)
                return 0

            lax.fori_loop(0, 4, body, 0)
            start(es[j])

        return event

    def ev_es(j):
        return es[j].wait_recv

    def probs_body(h, _):
        wr = rolled(h)
        scaled = wr * SCALE
        ws = [(scaled if l < 3 else wr)[:, 16 * l : 16 * l + 1] for l in range(7)]
        qh, kh = q_v[:, hcols(h)], k_v[:, hcols(h)]
        for blk in (0, 1):
            r0 = 256 * blk
            sc = dot(qh[r0 : r0 + 256], kh[r0 : r0 + 256], 1, 1)
            a, b = slice(r0, r0 + 128), slice(r0 + 128, r0 + 256)
            probs[h, blk, 0:128, 0:128] = (sc[:128, :128] * diag_mask(ws[0][a], ws[1][a])).astype(BF)
            probs[h, blk, 0:128, 128:256] = jnp.zeros((128, 128), BF)
            probs[h, blk, 128:256, 0:128] = (sc[128:, :128] * ws[2][b]).astype(BF)
            probs[h, blk, 128:256, 128:256] = (
                sc[128:, 128:] * diag_mask(ws[0][b], ws[1][b])
            ).astype(BF)
        qf = qh.astype(F32)
        for b in range(3):
            wq[h, :, 128 * b : 128 * b + 128] = (qf * ws[4 + b]).astype(BF)
        wq[h, 0:256, 384:512] = jnp.zeros((256, 128), BF)
        wq[h, 256:512, 384:512] = (qf[256:] * ws[3][256:]).astype(BF)
        return 0

    run(
        probs_body,
        [
            (1, ev_e0(0)), (2, ev_w(2, 0)), (4, ev_e0(1), ev_w(2, 1)), (11, ev_w(3, 0)),
            (14, ev_e1(0)), (16, ev_w(3, 1), ev_es(0)),
        ],
    )

    def attn_copy(h):
        return pltpu.make_async_remote_copy(
            src_ref=own_v.at[:, hcols(h)], dst_ref=attn_sib.at[h], send_sem=asem.at[h],
            recv_sem=arsem.at[h], device_id=sib, device_id_type=MESH,
        )

    def attn_body(i, _):
        hi, lo = chunked(i)
        h = hi * 8 + lo
        vh = v_v[:, hcols(h)]
        cross = dot(wq[h], far[hi, lo], 1, 0) * SCALE
        for blk in (0, 1):
            r0 = 256 * blk
            out = dot(probs[h, blk], vh[r0 : r0 + 256], 1, 0) + cross[r0 : r0 + 256]
            own_v[r0 : r0 + 256, hcols(h)] = out.astype(BF)
        attn_copy(h).start()
        return 0

    run(attn_body, [(4, ev_e1(1)), (8, ev_es(1)), (16, ev_w(4, 0))], step=2)

    loads[4].wait()
    dcopy.wait_recv()

    def wg_body(i, _):
        h = head(i)
        attn_copy(h).wait_recv()
        own = d_v[:, pl.ds(pl.multiple_of(core * HALF, HALF), HALF)]
        part = dot(own_v[:, hcols(h)], own, 0, 0) + dot(attn_sib[h], dosib[...], 0, 0)
        part = part.astype(BF)
        zd = rem(div(h, 4) + core, 4)
        cd = rem(div(h, 2), 2)
        for xi in (0, 1):
            xd = rem(2 * rem(h, 2) + xi + core, 4)
            for yi in range(4):
                yd = rem(yi + core, 4)
                row = (xi * 4 + yi) * 16
                for piece, (c0_, width) in enumerate(COLS):
                    accs[piece][zd, xd, yd, cd] = part[row : row + 16, c0_ : c0_ + width]
        return 0

    run(wg_body, [(13, ev_w(4, 1))])
    rs_start(0)

    for steps in wsteps:
        for i in (4, 5, 6):
            steps[i].wait_recv()

    def g_body(i, _):
        blocks = []
        hi, lo = chunked(2 * i)
        for j in (0, 1):
            h = hi * 8 + lo + j
            hx, hy = div(h, 4), rem(h, 4)
            hx1, hy1 = rem(hx + 1, 4), rem(hy + 1, 4)
            blocks += [w_g[0, 0, hx, hy], w_g[0, 1, hx1, hy1], w_g[1, 0, hy, hx], w_g[1, 1, hy1, hx1]]
        weight = jnp.concatenate(blocks, axis=0)
        out = dot(d_v[...], weight, 1, 1).astype(BF)
        for j in (0, 1):
            h = hi * 8 + lo + j
            gh = out[:, 128 * j : 128 * j + 128]
            g_v[h] = gh
            grads = dot(gh, wq[h], 0, 0)
            for b in range(3):
                gt[b, hi, lo + j] = (grads[:, 128 * b : 128 * b + 128] * (bit[b] * SCALE)).astype(BF)
            gt[3, hi, lo + j] = (grads[:, 384:512] * SCALE).astype(BF)
        return 0

    def ev_c12(j):
        def event():
            c12[j].wait_recv()

            def body(i, _):
                m = 4 * j + i
                for b in (0, 1):
                    both = gt[1 + b, core, m].astype(F32) + recv12[b, m].astype(F32)
                    cs12[b, m] = both.astype(BF)
                return 0

            lax.fori_loop(0, 4, body, 0)
            start(c1[j])
            start(c2[j])
            start(c3[j])

        return event

    def ev_c3(j):
        def event():
            c1[j].wait_recv()
            c2[j].wait_recv()
            c3[j].wait_recv()

            def body(i, _):
                m = 4 * j + i
                both = r1b[m].astype(F32) + r2b[m].astype(F32) + r3b[m].astype(F32)
                sgsum[core, m] = both.astype(BF)
                return 0

            lax.fori_loop(0, 4, body, 0)
            start(c4[j])

        return event

    run(
        g_body,
        [(4, starts(c0[0], c12[0])), (6, ev_c12(0)), (8, starts(c0[1], c12[1]))],
        count=H // 2,
    )

    def ev_rs(n):
        def event():
            rs_add(n)
            rs_start(n + 1)

        return event

    def wait_attn(h, _):
        attn_copy(h).wait_send()
        return 0

    lax.fori_loop(0, H, wait_attn, 0)
    tacc[...] = jnp.zeros_like(tacc)
    dsel = lax.broadcasted_iota(jnp.int32, (256, 128), 1) - 16 * div(
        lax.broadcasted_iota(jnp.int32, (256, 128), 0), 64
    )
    frow = lax.broadcasted_iota(jnp.int32, (512, 128), 0)
    dfar = lax.broadcasted_iota(jnp.int32, (512, 128), 1) - 64 - 16 * div(frow, 128)

    def dq_body(h, _):
        wr = rolled(h)
        ws = [wr[:, 16 * l : 16 * l + 1] for l in range(7)]
        qf = q_v[:, hcols(h)].astype(F32)
        kh, vh, gh = k_v[:, hcols(h)], v_v[:, hcols(h)], g_v[h]
        fh = far.at[div(h, 8), rem(h, 8)]
        sel = (dsel == h).astype(F32).astype(BF)
        fsel = (dfar == h).astype(F32).astype(BF)
        dq = None
        prods = []
        for b in range(3):
            pb = dot(gh, fh[128 * b : 128 * b + 128], 1, 1)
            prods.append((qf * pb).astype(BF))
            term = pb * ws[4 + b]
            dq = term if dq is None else dq + term
        p3 = dot(gh[256:], fh[384:512], 1, 1)
        prod3 = (qf[256:] * p3).astype(BF)
        p3 = p3 * ws[3][256:]
        for blk in (0, 1):
            r0 = 256 * blk
            pg = dot(gh[r0 : r0 + 256], vh[r0 : r0 + 256], 1, 1)
            a, b = slice(r0, r0 + 128), slice(r0 + 128, r0 + 256)
            top = jnp.concatenate(
                [(pg[:128, :128] * diag_mask(ws[0][a], ws[1][a])).astype(BF), jnp.zeros((128, 128), BF)], axis=1
            )
            bottom = jnp.concatenate(
                [
                    (pg[128:, :128] * ws[2][b]).astype(BF),
                    (pg[128:, 128:] * diag_mask(ws[0][b], ws[1][b])).astype(BF),
                ],
                axis=1,
            )
            sg = jnp.concatenate([top, bottom], axis=0)
            wq[h, r0 : r0 + 256, 0:256] = sg
            energy = (pg * probs[h, blk].astype(F32)).astype(BF)
            out = dot(sg, kh[r0 : r0 + 256], 1, 0) + dq[r0 : r0 + 256]
            fars = [prods[b][r0 : r0 + 256] for b in range(3)]
            if blk == 1:
                out = out + p3
                fars.append(prod3)
                sums = dot(jnp.concatenate(fars, axis=1), fsel, 1, 0)
            else:
                sums = dot(jnp.concatenate(fars, axis=1), fsel[:384], 1, 0)
            own_v[r0 : r0 + 256, hcols(h)] = (out * SCALE).astype(BF)
            tacc[r0 : r0 + 256] += sums + dot(energy, sel, 1, 0)
        return 0

    run(
        dq_body,
        [
            (2, ev_rs(0)), (3, ev_c12(1)), (6, ev_c3(0)), (9, ev_rs(1)), (13, ev_c3(1)),
            (14, ev_rs(2)),
        ],
    )
    for j in (0, 1):
        c0[j].wait_recv()
        c4[j].wait_recv()

    def dk_body(h, _):
        hi, lo = div(h, 8), rem(h, 8)
        base = sg0[hi, lo].astype(F32) + sgsum[hi, lo].astype(F32)
        halves = ((base + gt[3, hi, lo].astype(F32)).astype(BF), base.astype(BF))
        for blk in (0, 1):
            rows = pl.ds(256 * blk, 256)
            kb, vb, qb = k_v[rows, hcols(h)], v_v[rows, hcols(h)], q_v[rows, hcols(h)]
            gb = g_v[h, rows]
            dv = dot(probs[h, blk], gb, 0, 0) + dot(kb, halves[blk], 1, 1)
            dk = dot(wq[h, rows, 0:256], qb, 0, 0) * SCALE + dot(vb, halves[blk], 1, 0)
            k_v[rows, hcols(h)] = dk.astype(BF)
            v_v[rows, hcols(h)] = dv.astype(BF)
        return 0

    def finish():
        for piece, (first, width) in enumerate(COLS):
            rs_copies[piece][5].wait_recv()
            f32s, recv = kept[piece], recvs[piece][5]
            at = tuple(s.start for s in rs_kept[piece][5])
            cols = slice(first, first + width)
            wgout[core, :, cols] = f32s[at + (core,)] + recv[0, 0, 0, core].astype(F32)
            finsend[:, cols] = f32s[at + (1 - core,)] + recv[0, 0, 0, 1 - core].astype(F32)
        start(last)

    last = remote(50, finsend, wgout.at[core], sib)
    run(dk_body, [(4, ev_rs(3)), (10, ev_rs(4)), (16, finish)], step=2)

    lane = lax.broadcasted_iota(jnp.int32, (64, 128), 1)
    for i in range(8):
        rows = slice(64 * i, 64 * i + 64)
        g4 = i % 4
        t = tacc[rows]

        def moved(frm, to, t=t):
            shift = (to - frm) * 16 % 128
            return pltpu.roll(t, shift, 1) if shift else t

        res = jnp.where(lane < 16, moved(g4, 0), 0.0)
        if g4 % 2 == 1:
            res = jnp.where((lane >= 16) & (lane < 32), moved(g4 - 1, 1), res)
        if g4 >= 2:
            res = jnp.where((lane >= 32) & (lane < 48), moved(0, 2) + moved(1, 2), res)
        res = res / gain_v[rows]
        if i >= 4:
            res = jnp.where((lane >= 48) & (lane < 64), moved(7, 3) * SCALE, res)
        res = jnp.where((lane >= 64) & (lane < 112), t * SCALE, res)
        tacc[rows] = res
    last.wait_recv()
    for i in (0, 1):
        wg_out[:, HALF * i : HALF * i + HALF] = wgout[i]
    for c in sent:
        c.wait_send()


def local(queries, keys, values, level_gain, out_weight, out_grad):
    big = pltpu.VMEM((1, T, D), BF)
    state = (2, 8, HD, HD)
    scratch = [
        pltpu.VMEM((T, D), BF),
        pltpu.VMEM((T, D), BF),
        pltpu.VMEM((T, HD), F32),
        pltpu.VMEM((2, 2, 4, 4, 32, D), BF),
        pltpu.VMEM((H, T, HD), BF),
        pltpu.VMEM((T, HALF), BF),
        pltpu.VMEM((H, T, T), BF),
        pltpu.VMEM((H, 2, 256, 256), BF),
        pltpu.VMEM((H, T, HD), BF),
        pltpu.VMEM((2, 8, T, HD), BF),
        pltpu.VMEM(state, F32),
        pltpu.VMEM(state, F32),
        pltpu.VMEM((8, HD, HD), BF),
        pltpu.VMEM((8, HD, HD), BF),
        pltpu.VMEM((8, HD, HD), BF),
        pltpu.VMEM((8, HD, HD), BF),
        pltpu.VMEM((4,) + state, BF),
        pltpu.VMEM(state, BF),
        pltpu.VMEM(state, BF),
        pltpu.VMEM(state, BF),
        pltpu.VMEM((8, HD, HD), BF),
        pltpu.VMEM((8, HD, HD), BF),
        pltpu.VMEM((8, HD, HD), BF),
        pltpu.VMEM(state, BF),
        pltpu.VMEM((2, 16, HALF), F32),
        pltpu.VMEM((16, HALF), F32),
    ]
    scratch += [pltpu.VMEM((4, 4, 4, 2, 16, width), BF) for _, width in COLS]
    scratch += [pltpu.VMEM(shape, F32) for shape in recv_shapes()[::6]]
    scratch += [pltpu.VMEM(shape, BF) for shape in recv_shapes()]
    scratch += [
        pltpu.SemaphoreType.DMA((8,)),
        pltpu.SemaphoreType.DMA((112,)),
        pltpu.SemaphoreType.DMA((112,)),
        pltpu.SemaphoreType.DMA((H,)),
        pltpu.SemaphoreType.DMA((H,)),
    ]
    anyspace = pl.BlockSpec(memory_space=pl.ANY)
    return pl.pallas_call(
        kernel,
        out_shape=(
            big, big, big,
            pltpu.VMEM((1, T, HD), F32),
            pltpu.VMEM((16, D), F32),
        ),
        in_specs=[anyspace] * 6,
        out_specs=(pl.BlockSpec(memory_space=pltpu.VMEM),) * 5,
        scratch_shapes=scratch,
        compiler_params=pltpu.CompilerParams(
            collective_id=0, has_side_effects=True, vmem_limit_bytes=57 * 2**20
        ),
        cost_estimate=pl.CostEstimate(flops=20 * 10**9, bytes_accessed=16 * 2**20, transcendentals=0),
    )(queries, keys, values, level_gain, out_weight, out_grad)


def solution(mesh):
    tokens = P("batch", "seq", None)
    return jax.shard_map(
        local,
        mesh=mesh,
        in_specs=(tokens, tokens, tokens, tokens, P("batch", None), tokens),
        out_specs=(tokens, tokens, tokens, tokens, P(("seq", "batch"), None)),
        check_vma=False,
    )
```

```python
import jax
import jax.numpy as jnp
from jax import lax
from jax.experimental import pallas as pl
from jax.experimental.pallas import tpu as pltpu
from jax.sharding import PartitionSpec as P

H = 16
HD = 128
T = 512
D = 2048
HALF = 1024
SCALE = HD**-0.5
BF = jnp.bfloat16
F32 = jnp.float32
MESH = pl.DeviceIdType.MESH
COLS = ((0, 384), (384, 384), (768, 256))
ORDERS = ((1, 2, 0), (2, 0, 1), (0, 1, 2))


def dot(a, b, ca, cb):
    return lax.dot_general(a, b, (((ca,), (cb,)), ((), ())), preferred_element_type=F32)


def rem(a, b):
    return lax.rem(a, jnp.int32(b))


def div(a, b):
    return lax.div(a, jnp.int32(b))


def flip(a):
    return a + 1 - 2 * rem(a, 2)


def recv_shapes():
    shapes = []
    for piece, (_, width) in enumerate(COLS):
        dims = [4, 4, 4]
        for axis in ORDERS[piece]:
            for left in (2, 1):
                dims[axis] = left
                shapes.append(tuple(dims) + (2, 16, width))
    return shapes


def kernel(
    q_in, k_in, v_in, gain_in, w_in, d_in,
    dq_out, dk_out, dv_out, gain_out, wg_out,
    q_v, d_v, gain_v, w_g, attn_sib, dosib, wq, probs, g_v, far,
    st, st_sib, cs_send, r1, r2, r3,
    gt, sg0, recv12, cs12, r1b, r2b, r3b, sgsum, wgout, finsend,
    acc0, acc1, acc2, fk0, fk1, fk2,
    *rest,
):
    recvs = [rest[0:6], rest[6:12], rest[12:18]]
    lsem, ssem, rsem, asem, arsem = rest[18:]
    accs = (acc0, acc1, acc2)
    kept = (fk0, fk1, fk2)
    k_v, v_v, own_v, tacc = dk_out.at[0], dv_out.at[0], dq_out.at[0], gain_out.at[0]
    seq = lax.axis_index("seq")
    bat = lax.axis_index("batch")
    core, z = rem(seq, 2), div(seq, 2)
    x, y = div(bat, 4), rem(bat, 4)
    sib = (z * 2 + 1 - core, bat)

    def load(i, src, dst):
        return pltpu.make_async_copy(src, dst, lsem.at[i])

    loads = [
        load(0, k_in.at[0], k_v),
        load(1, v_in.at[0], v_v),
        load(2, q_in.at[0], q_v),
        load(3, gain_in.at[0], gain_v),
        load(4, d_in.at[0], d_v),
    ]

    a1 = x * (1 - core) + y * core
    a2 = y * (1 - core) + x * core
    wloads, wsteps = [], []
    for p in (0, 1):
        b1, b2 = rem(a1 + p, 4), rem(a2 + p, 4)

        def dev(c1, c2, p=p):
            o1, o2 = rem(c1 + 4 - p, 4), rem(c2 + 4 - p, 4)
            return (seq, (o1 * 4 + o2) * (1 - core) + (o2 * 4 + o1) * core)

        own32 = w_in.at[pl.ds(pl.multiple_of(core * 64 + p * 32, 32), 32), :]
        wloads.append(load(5 + p, own32, w_g.at[core, p, b1, b2]))
        pair1, pair2 = div(b1, 2) * 2, div(b2, 2) * 2
        for k in (0, 1):
            sub = pl.ds(16 * k, 16)
            own = w_in.at[pl.ds(pl.multiple_of(core * 64 + p * 32 + k * 16, 16), 16), :]
            steps = []

            def add(src, dst, device, base=80 + (p * 2 + k) * 7, steps=steps):
                i = base + len(steps)
                steps.append(
                    pltpu.make_async_remote_copy(
                        src_ref=src, dst_ref=dst, send_sem=ssem.at[i], recv_sem=rsem.at[i],
                        device_id=device, device_id_type=MESH,
                    )
                )

            add(own, w_g.at[core, p, b1, b2, sub], dev(flip(b1), b2))
            two = w_g.at[core, p, pl.ds(pair1, 2), b2, sub]
            add(two, two, dev(3 - b1, b2))
            four = w_g.at[core, p, :, b2, sub]
            add(four, four, dev(b1, flip(b2)))
            eight = w_g.at[core, p, :, pl.ds(pair2, 2), sub]
            add(eight, eight, dev(b1, 3 - b2))
            add(four, four, sib)
            four2 = w_g.at[core, p, :, flip(b2), sub]
            add(four2, four2, sib)
            eight2 = w_g.at[core, p, :, pl.ds(2 - pair2, 2), sub]
            add(eight2, eight2, sib)
            wsteps.append(steps)
    for c in wloads + loads[:2]:
        c.start()

    barrier = pltpu.get_barrier_semaphore()
    neighbours = [
        sib,
        (seq, flip(x) * 4 + y), (seq, (3 - x) * 4 + y),
        (seq, x * 4 + flip(y)), (seq, x * 4 + 3 - y),
        (flip(z) * 2 + core, bat), ((3 - z) * 2 + core, bat), (rem(z + 2, 4) * 2 + core, bat),
    ]
    for n in neighbours:
        pl.semaphore_signal(barrier, inc=1, device_id=n, device_id_type=MESH)
    pl.semaphore_wait(barrier, len(neighbours))

    def remote(i, src, dst, device):
        return pltpu.make_async_remote_copy(
            src_ref=src, dst_ref=dst, send_sem=ssem.at[i], recv_sem=rsem.at[i],
            device_id=device, device_id_type=MESH,
        )

    sent = []

    def start(c):
        c.start()
        sent.append(c)

    for k in (0, 1):
        for p in (0, 1):
            start(wsteps[2 * p + k][0])

    dcopy = remote(
        20, d_in.at[0, :, pl.ds(pl.multiple_of((1 - core) * HALF, HALF), HALF)], dosib, sib
    )

    zp1 = (flip(z) * 2 + core, bat)
    zp3 = ((3 - z) * 2 + core, bat)
    zp2 = (rem(z + 2, 4) * 2 + core, bat)
    e0, e1, e2, e3, es, c0, c12, c1, c2, c3, c4 = [[] for _ in range(11)]
    for j in (0, 1):
        four = pl.ds(4 * j, 4)
        n = 51 + 11 * j
        e0.append(remote(n, st.at[:, four], st_sib.at[:, four], sib))
        e1.append(remote(n + 1, cs_send.at[four], r1.at[four], zp1))
        e2.append(remote(n + 2, cs_send.at[four], r2.at[four], zp3))
        e3.append(remote(n + 10, cs_send.at[four], r3.at[four], zp2))
        fars = far.at[core, four, pl.ds(128, 256)]
        es.append(remote(n + 3, fars, fars, sib))
        c0.append(remote(n + 4, gt.at[0, :, four], sg0.at[:, four], sib))
        c12.append(remote(n + 5, gt.at[pl.ds(1, 2), 1 - core, four], recv12.at[:, four], sib))
        c1.append(remote(n + 6, cs12.at[0, four], r1b.at[four], zp1))
        c2.append(remote(n + 7, cs12.at[1, four], r2b.at[four], zp3))
        c3.append(remote(n + 8, cs12.at[1, four], r3b.at[four], zp2))
        sums = sgsum.at[core, four]
        c4.append(remote(n + 9, sums, sums, sib))
    bit = [rem(seq, 2).astype(F32), rem(z, 2).astype(F32), div(z, 2).astype(F32)]

    rot = [rem(z + core, 4), rem(x + core, 4), rem(y + core, 4)]

    def axis_dev(axis, r):
        o = rem(r + 4 - core, 4)
        if axis == 0:
            return (o * 2 + core, bat)
        if axis == 1:
            return (seq, o * 4 + y)
        return (seq, x * 4 + o)

    rs_copies, rs_keeps, rs_kept = [], [], []
    for piece in range(3):
        copies, keeps, local_keeps = [], [], []
        cur = [pl.ds(0, 4)] * 3
        cur_local = [pl.ds(0, 4)] * 3
        for axis in ORDERS[piece]:
            a = rot[axis]
            for sub in (0, 1):
                give, keep = list(cur), list(cur)
                if sub == 0:
                    give[axis] = pl.ds(2 - 2 * div(a, 2), 2)
                    keep[axis] = pl.ds(2 * div(a, 2), 2)
                    to = axis_dev(axis, 3 - a)
                else:
                    give[axis] = pl.ds(flip(a), 1)
                    keep[axis] = pl.ds(a, 1)
                    to = axis_dev(axis, flip(a))
                n = len(copies)
                copies.append(
                    remote(32 + piece * 6 + n, accs[piece].at[tuple(give)], recvs[piece][n], to)
                )
                keeps.append(tuple(keep))
                cur = keep
                if axis == ORDERS[piece][0]:
                    cur_local[axis] = pl.ds(0, 2) if sub == 0 else pl.ds(rem(a, 2), 1)
                else:
                    cur_local[axis] = keep[axis]
                local_keeps.append(tuple(cur_local))
        rs_copies.append(copies)
        rs_keeps.append(keeps)
        rs_kept.append(local_keeps)

    def rs_start(n):
        for piece in range(3):
            start(rs_copies[piece][n])

    def rs_add(n):
        for piece in range(3):
            rs_copies[piece][n].wait_recv()
            keep, local_keep = rs_keeps[piece][n], rs_kept[piece][n]
            recv, acc, f32s = recvs[piece][n], accs[piece], kept[piece]

            def body(i, _, keep=keep, local_keep=local_keep, recv=recv, acc=acc, f32s=f32s):
                at = (keep[0].start + i,) + keep[1:]
                local_at = (local_keep[0].start + i,) + local_keep[1:]
                before = acc[at].astype(F32) if n == 0 else f32s[local_at]
                value = before + recv[i].astype(F32)
                f32s[local_at] = value
                acc[at] = value.astype(BF)
                return 0

            lax.fori_loop(0, keep[0].size, body, 0)

    def hcols(h):
        return pl.ds(pl.multiple_of(h * HD, HD), HD)

    def rolled(h):
        return pltpu.roll(gain_v[...], rem(jnp.int32(HD) - h, HD), 1)

    loads[0].wait()
    loads[1].wait()
    for c in loads[2:]:
        c.start()
    start(dcopy)

    def chunked(i):
        j, r = div(i, 8), rem(i, 8)
        return div(r, 4), 4 * j + rem(r, 4)

    def head(i):
        hi, lo = chunked(i)
        return hi * 8 + lo

    def state_body(i, _):
        hi, lo = chunked(i)
        h = hi * 8 + lo
        kh, vh = k_v[:, hcols(h)], v_v[:, hcols(h)]
        low = dot(kh[:256], vh[:256], 0, 0)
        far[hi, lo, 384:512] = low.astype(BF)
        st[hi, lo] = low + dot(kh[256:], vh[256:], 0, 0)
        return 0

    def ev_w(n, k):
        def event():
            for p in (0, 1):
                steps = wsteps[2 * p + k]
                if n == 1 and k == 0:
                    wloads[p].wait()
                steps[n - 1].wait_recv()
                if n < 4:
                    start(steps[n])
                if n > 1:
                    start(steps[n + 2])

        return event

    def run(body, cuts, count=H, step=1):
        def stepped(i, _):
            for at, *events in cuts:
                if at < count:

                    @pl.when(i * step == at)
                    def _():
                        for event in events:
                            event()

            for j in range(step):
                body(i * step + j, 0)
            return 0

        lax.fori_loop(0, count // step, stepped, 0)
        for at, *events in cuts:
            if at >= count:
                for event in events:
                    event()

    def starts(*copies):
        def event():
            for c in copies:
                start(c)

        return event

    run(
        state_body,
        [(4, ev_w(1, 0)), (8, starts(e0[0]), ev_w(1, 1)), (16, starts(e0[1]))],
        step=2,
    )
    loads[2].wait()
    loads[3].wait()

    rr = lax.broadcasted_iota(jnp.int32, (128, 128), 0)
    cc = lax.broadcasted_iota(jnp.int32, (128, 128), 1)
    same = (rr < 64) == (cc < 64)
    m0 = (rr >= cc) & same
    m1 = (rr >= 64) & (cc < 64)

    def diag_mask(w0, w1):
        return jnp.where(m0, w0, jnp.where(m1, w1, 0.0))

    def ev_e0(j):
        def event():
            e0[j].wait_recv()

            def body(i, _):
                m = 4 * j + i
                for hi in (0, 1):
                    far[hi, m, 0:128] = (st_sib[hi, m] * bit[0]).astype(BF)
                cs_send[m] = (st[core, m] + st_sib[core, m]).astype(BF)
                return 0

            lax.fori_loop(0, 4, body, 0)
            start(e1[j])
            start(e2[j])
            start(e3[j])

        return event

    def ev_e1(j):
        def event():
            e1[j].wait_recv()
            e2[j].wait_recv()
            e3[j].wait_recv()

            def body(i, _):
                m = 4 * j + i
                far[core, m, 128:256] = (r1[m].astype(F32) * bit[1]).astype(BF)
                far[core, m, 256:384] = ((r2[m].astype(F32) + r3[m].astype(F32)) * bit[2]).astype(BF)
                return 0

            lax.fori_loop(0, 4, body, 0)
            start(es[j])

        return event

    def ev_es(j):
        return es[j].wait_recv

    def probs_body(h, _):
        wr = rolled(h)
        scaled = wr * SCALE
        ws = [(scaled if l < 3 else wr)[:, 16 * l : 16 * l + 1] for l in range(7)]
        qh, kh = q_v[:, hcols(h)], k_v[:, hcols(h)]
        for t in range(4):
            blk, r0, c0_ = t // 2, 128 * t, 256 * (t // 2)
            rows, inner = slice(r0, r0 + 128), slice(r0 - c0_, r0 - c0_ + 128)
            sc = dot(qh[rows], kh[c0_ : r0 + 128], 1, 1)
            diag = sc[:, -128:] * diag_mask(ws[0][rows], ws[1][rows])
            probs[h, blk, inner, inner] = diag.astype(BF)
            if t % 2 == 1:
                probs[h, blk, inner, 0:128] = (sc[:, :128] * ws[2][rows]).astype(BF)
        qf = qh.astype(F32)
        for b in range(3):
            wq[h, :, 128 * b : 128 * b + 128] = (qf * ws[4 + b]).astype(BF)
        wq[h, 0:256, 384:512] = jnp.zeros((256, 128), BF)
        wq[h, 256:512, 384:512] = (qf[256:] * ws[3][256:]).astype(BF)
        return 0

    run(
        probs_body,
        [
            (1, ev_e0(0)), (2, ev_w(2, 0)), (4, ev_e0(1), ev_w(2, 1)), (11, ev_w(3, 0)),
            (14, ev_e1(0)), (16, ev_w(3, 1), ev_es(0)),
        ],
    )

    def attn_copy(h):
        return pltpu.make_async_remote_copy(
            src_ref=own_v.at[:, hcols(h)], dst_ref=attn_sib.at[h], send_sem=asem.at[h],
            recv_sem=arsem.at[h], device_id=sib, device_id_type=MESH,
        )

    def attn_body(i, _):
        hi, lo = chunked(i)
        h = hi * 8 + lo
        vh = v_v[:, hcols(h)]
        cross = dot(wq[h], far[hi, lo], 1, 0) * SCALE
        for t in range(4):
            blk, r0, c0_ = t // 2, 128 * t, 256 * (t // 2)
            near = probs[h, blk, r0 - c0_ : r0 - c0_ + 128, 0 : r0 - c0_ + 128]
            out = dot(near, vh[c0_ : r0 + 128], 1, 0) + cross[r0 : r0 + 128]
            own_v[r0 : r0 + 128, hcols(h)] = out.astype(BF)
        attn_copy(h).start()
        return 0

    run(attn_body, [(4, ev_e1(1)), (8, ev_es(1)), (16, ev_w(4, 0))], step=2)

    loads[4].wait()
    dcopy.wait_recv()

    def wg_body(i, _):
        h = head(i)
        attn_copy(h).wait_recv()
        own = d_v[:, pl.ds(pl.multiple_of(core * HALF, HALF), HALF)]
        part = dot(own_v[:, hcols(h)], own, 0, 0) + dot(attn_sib[h], dosib[...], 0, 0)
        part = part.astype(BF)
        zd = rem(div(h, 4) + core, 4)
        cd = rem(div(h, 2), 2)
        for xi in (0, 1):
            xd = rem(2 * rem(h, 2) + xi + core, 4)
            for yi in range(4):
                yd = rem(yi + core, 4)
                row = (xi * 4 + yi) * 16
                for piece, (c0_, width) in enumerate(COLS):
                    accs[piece][zd, xd, yd, cd] = part[row : row + 16, c0_ : c0_ + width]
        return 0

    run(wg_body, [(13, ev_w(4, 1))])
    rs_start(0)

    for steps in wsteps:
        for i in (4, 5, 6):
            steps[i].wait_recv()

    def g_body(i, _):
        blocks = []
        hi, lo = chunked(2 * i)
        for j in (0, 1):
            h = hi * 8 + lo + j
            hx, hy = div(h, 4), rem(h, 4)
            hx1, hy1 = rem(hx + 1, 4), rem(hy + 1, 4)
            blocks += [w_g[0, 0, hx, hy], w_g[0, 1, hx1, hy1], w_g[1, 0, hy, hx], w_g[1, 1, hy1, hx1]]
        weight = jnp.concatenate(blocks, axis=0)
        out = dot(d_v[...], weight, 1, 1).astype(BF)
        for j in (0, 1):
            h = hi * 8 + lo + j
            gh = out[:, 128 * j : 128 * j + 128]
            g_v[h] = gh
            grads = dot(gh, wq[h], 0, 0)
            for b in range(3):
                gt[b, hi, lo + j] = (grads[:, 128 * b : 128 * b + 128] * (bit[b] * SCALE)).astype(BF)
            gt[3, hi, lo + j] = (grads[:, 384:512] * SCALE).astype(BF)
        return 0

    def ev_c12(j):
        def event():
            c12[j].wait_recv()

            def body(i, _):
                m = 4 * j + i
                for b in (0, 1):
                    both = gt[1 + b, core, m].astype(F32) + recv12[b, m].astype(F32)
                    cs12[b, m] = both.astype(BF)
                return 0

            lax.fori_loop(0, 4, body, 0)
            start(c1[j])
            start(c2[j])
            start(c3[j])

        return event

    def ev_c3(j):
        def event():
            c1[j].wait_recv()
            c2[j].wait_recv()
            c3[j].wait_recv()

            def body(i, _):
                m = 4 * j + i
                both = r1b[m].astype(F32) + r2b[m].astype(F32) + r3b[m].astype(F32)
                sgsum[core, m] = both.astype(BF)
                return 0

            lax.fori_loop(0, 4, body, 0)
            start(c4[j])

        return event

    def ev_rs(n):
        def event():
            rs_add(n)
            rs_start(n + 1)

        return event

    run(
        g_body,
        [(4, starts(c0[0], c12[0])), (6, ev_c12(0)), (8, starts(c0[1], c12[1]), ev_rs(0))],
        count=H // 2,
    )

    def wait_attn(h, _):
        attn_copy(h).wait_send()
        return 0

    lax.fori_loop(0, H, wait_attn, 0)
    tacc[...] = jnp.zeros_like(tacc)
    dsel = lax.broadcasted_iota(jnp.int32, (256, 128), 1) - 16 * div(
        lax.broadcasted_iota(jnp.int32, (256, 128), 0), 64
    )
    frow = lax.broadcasted_iota(jnp.int32, (512, 128), 0)
    dfar = lax.broadcasted_iota(jnp.int32, (512, 128), 1) - 64 - 16 * div(frow, 128)

    def dq_body(h, _):
        wr = rolled(h)
        ws = [wr[:, 16 * l : 16 * l + 1] for l in range(7)]
        qf = q_v[:, hcols(h)].astype(F32)
        kh, vh, gh = k_v[:, hcols(h)], v_v[:, hcols(h)], g_v[h]
        fh = far.at[div(h, 8), rem(h, 8)]
        sel = (dsel == h).astype(F32).astype(BF)
        fsel = (dfar == h).astype(F32).astype(BF)
        dq = None
        prods = []
        for b in range(3):
            pb = dot(gh, fh[128 * b : 128 * b + 128], 1, 1)
            prods.append((qf * pb).astype(BF))
            term = pb * ws[4 + b]
            dq = term if dq is None else dq + term
        p3 = dot(gh[256:], fh[384:512], 1, 1)
        prod3 = (qf[256:] * p3).astype(BF)
        p3 = p3 * ws[3][256:]
        far_sums = []
        for blk in (0, 1):
            r0 = 256 * blk
            fars = [prods[b][r0 : r0 + 256] for b in range(3)]
            if blk == 1:
                fars.append(prod3)
                sums = dot(jnp.concatenate(fars, axis=1), fsel, 1, 0)
            else:
                sums = dot(jnp.concatenate(fars, axis=1), fsel[:384], 1, 0)
            far_sums.append(sums)
        for t in range(4):
            blk, r0, c0_ = t // 2, 128 * t, 256 * (t // 2)
            rows, inner = slice(r0, r0 + 128), slice(r0 - c0_, r0 - c0_ + 128)
            width = r0 - c0_ + 128
            pg = dot(gh[rows], vh[c0_ : r0 + 128], 1, 1)
            sg = (pg[:, -128:] * diag_mask(ws[0][rows], ws[1][rows])).astype(BF)
            if t % 2 == 1:
                sg = jnp.concatenate([(pg[:, :128] * ws[2][rows]).astype(BF), sg], axis=1)
            wq[h, rows, 0:width] = sg
            energy = (pg * probs[h, blk, inner, 0:width].astype(F32)).astype(BF)
            out = dot(sg, kh[c0_ : r0 + 128], 1, 0) + dq[rows]
            if blk == 1:
                out = out + p3[inner]
            own_v[rows, hcols(h)] = (out * SCALE).astype(BF)
            tacc[rows] += far_sums[blk][inner] + dot(energy, sel[:width], 1, 0)
        return 0

    run(
        dq_body,
        [
            (2, ev_c12(1)), (5, ev_c3(0)), (7, ev_rs(1)), (12, ev_rs(2)), (13, ev_c3(1)),
            (16, ev_rs(3)),
        ],
    )
    for j in (0, 1):
        c0[j].wait_recv()
        c4[j].wait_recv()

    def dk_body(h, _):
        hi, lo = div(h, 8), rem(h, 8)
        base = sg0[hi, lo].astype(F32) + sgsum[hi, lo].astype(F32)
        halves = ((base + gt[3, hi, lo].astype(F32)).astype(BF), base.astype(BF))
        for blk in (0, 1):
            for r0 in (256 * blk, 256 * blk + 128):
                rows, after = slice(r0, r0 + 128), slice(r0, 256 * blk + 256)
                inner = slice(r0 - 256 * blk, r0 - 256 * blk + 128)
                kb, vb = k_v[rows, hcols(h)], v_v[rows, hcols(h)]
                dv = dot(probs[h, blk, inner.start : 256, inner], g_v[h, after], 0, 0)
                dk = dot(wq[h, after, inner], q_v[after, hcols(h)], 0, 0)
                k_v[rows, hcols(h)] = (dk * SCALE + dot(vb, halves[blk], 1, 0)).astype(BF)
                v_v[rows, hcols(h)] = (dv + dot(kb, halves[blk], 1, 1)).astype(BF)
        return 0

    def finish():
        for piece, (first, width) in enumerate(COLS):
            rs_copies[piece][5].wait_recv()
            f32s, recv = kept[piece], recvs[piece][5]
            at = tuple(s.start for s in rs_kept[piece][5])
            cols = slice(first, first + width)
            wgout[core, :, cols] = f32s[at + (core,)] + recv[0, 0, 0, core].astype(F32)
            finsend[:, cols] = f32s[at + (1 - core,)] + recv[0, 0, 0, 1 - core].astype(F32)
        start(last)

    last = remote(50, finsend, wgout.at[core], sib)
    run(dk_body, [(6, ev_rs(4)), (14, finish)], step=2)

    lane = lax.broadcasted_iota(jnp.int32, (64, 128), 1)
    for i in range(8):
        rows = slice(64 * i, 64 * i + 64)
        g4 = i % 4
        t = tacc[rows]

        def moved(frm, to, t=t):
            shift = (to - frm) * 16 % 128
            return pltpu.roll(t, shift, 1) if shift else t

        res = jnp.where(lane < 16, moved(g4, 0), 0.0)
        if g4 % 2 == 1:
            res = jnp.where((lane >= 16) & (lane < 32), moved(g4 - 1, 1), res)
        if g4 >= 2:
            res = jnp.where((lane >= 32) & (lane < 48), moved(0, 2) + moved(1, 2), res)
        res = res / gain_v[rows]
        if i >= 4:
            res = jnp.where((lane >= 48) & (lane < 64), moved(7, 3) * SCALE, res)
        res = jnp.where((lane >= 64) & (lane < 112), t * SCALE, res)
        tacc[rows] = res
    last.wait_recv()
    for i in (0, 1):
        wg_out[:, HALF * i : HALF * i + HALF] = wgout[i]
    for c in sent:
        c.wait_send()


def local(queries, keys, values, level_gain, out_weight, out_grad):
    big = pltpu.VMEM((1, T, D), BF)
    state = (2, 8, HD, HD)
    scratch = [
        pltpu.VMEM((T, D), BF),
        pltpu.VMEM((T, D), BF),
        pltpu.VMEM((T, HD), F32),
        pltpu.VMEM((2, 2, 4, 4, 32, D), BF),
        pltpu.VMEM((H, T, HD), BF),
        pltpu.VMEM((T, HALF), BF),
        pltpu.VMEM((H, T, T), BF),
        pltpu.VMEM((H, 2, 256, 256), BF),
        pltpu.VMEM((H, T, HD), BF),
        pltpu.VMEM((2, 8, T, HD), BF),
        pltpu.VMEM(state, F32),
        pltpu.VMEM(state, F32),
        pltpu.VMEM((8, HD, HD), BF),
        pltpu.VMEM((8, HD, HD), BF),
        pltpu.VMEM((8, HD, HD), BF),
        pltpu.VMEM((8, HD, HD), BF),
        pltpu.VMEM((4,) + state, BF),
        pltpu.VMEM(state, BF),
        pltpu.VMEM(state, BF),
        pltpu.VMEM(state, BF),
        pltpu.VMEM((8, HD, HD), BF),
        pltpu.VMEM((8, HD, HD), BF),
        pltpu.VMEM((8, HD, HD), BF),
        pltpu.VMEM(state, BF),
        pltpu.VMEM((2, 16, HALF), F32),
        pltpu.VMEM((16, HALF), F32),
    ]
    scratch += [pltpu.VMEM((4, 4, 4, 2, 16, width), BF) for _, width in COLS]
    scratch += [pltpu.VMEM(shape, F32) for shape in recv_shapes()[::6]]
    scratch += [pltpu.VMEM(shape, BF) for shape in recv_shapes()]
    scratch += [
        pltpu.SemaphoreType.DMA((8,)),
        pltpu.SemaphoreType.DMA((112,)),
        pltpu.SemaphoreType.DMA((112,)),
        pltpu.SemaphoreType.DMA((H,)),
        pltpu.SemaphoreType.DMA((H,)),
    ]
    anyspace = pl.BlockSpec(memory_space=pl.ANY)
    return pl.pallas_call(
        kernel,
        out_shape=(
            big, big, big,
            pltpu.VMEM((1, T, HD), F32),
            pltpu.VMEM((16, D), F32),
        ),
        in_specs=[anyspace] * 6,
        out_specs=(pl.BlockSpec(memory_space=pltpu.VMEM),) * 5,
        scratch_shapes=scratch,
        compiler_params=pltpu.CompilerParams(
            collective_id=0, has_side_effects=True, vmem_limit_bytes=57 * 2**20
        ),
        cost_estimate=pl.CostEstimate(flops=20 * 10**9, bytes_accessed=16 * 2**20, transcendentals=0),
    )(queries, keys, values, level_gain, out_weight, out_grad)


def solution(mesh):
    tokens = P("batch", "seq", None)
    return jax.shard_map(
        local,
        mesh=mesh,
        in_specs=(tokens, tokens, tokens, tokens, P("batch", None), tokens),
        out_specs=(tokens, tokens, tokens, tokens, P(("seq", "batch"), None)),
        check_vma=False,
    )
```

```python
import jax
import jax.numpy as jnp
from jax import lax
from jax.experimental import pallas as pl
from jax.experimental.pallas import tpu as pltpu
from jax.sharding import PartitionSpec as P

H = 16
HD = 128
T = 512
D = 2048
HALF = 1024
SCALE = HD**-0.5
BF = jnp.bfloat16
F32 = jnp.float32
MESH = pl.DeviceIdType.MESH
COLS = ((0, 384), (384, 384), (768, 256))
ORDERS = ((1, 2, 0), (2, 0, 1), (0, 1, 2))


def dot(a, b, ca, cb):
    return lax.dot_general(a, b, (((ca,), (cb,)), ((), ())), preferred_element_type=F32)


def rem(a, b):
    return lax.rem(a, jnp.int32(b))


def div(a, b):
    return lax.div(a, jnp.int32(b))


def flip(a):
    return a + 1 - 2 * rem(a, 2)


def recv_shapes():
    shapes = []
    for piece, (_, width) in enumerate(COLS):
        dims = [4, 4, 4]
        for axis in ORDERS[piece]:
            for left in (2, 1):
                dims[axis] = left
                shapes.append(tuple(dims) + (2, 16, width))
    return shapes


def kernel(
    q_in, k_in, v_in, gain_in, w_in, d_in,
    dq_out, dk_out, dv_out, gain_out, wg_out,
    q_v, d_v, gain_v, w_g, attn_sib, dosib, wq, probs, g_v, far,
    st, st_sib, cs_send, r1, r2, r3,
    gt, sg0, recv12, cs12, r1b, r2b, r3b, sgsum, wgout, finsend,
    acc0, acc1, acc2, fk0, fk1, fk2,
    *rest,
):
    recvs = [rest[0:6], rest[6:12], rest[12:18]]
    lsem, ssem, rsem, asem, arsem = rest[18:]
    accs = (acc0, acc1, acc2)
    kept = (fk0, fk1, fk2)
    k_v, v_v, own_v, tacc = dk_out.at[0], dv_out.at[0], dq_out.at[0], gain_out.at[0]
    seq = lax.axis_index("seq")
    bat = lax.axis_index("batch")
    core, z = rem(seq, 2), div(seq, 2)
    x, y = div(bat, 4), rem(bat, 4)
    sib = (z * 2 + 1 - core, bat)

    def load(i, src, dst):
        return pltpu.make_async_copy(src, dst, lsem.at[i])

    loads = [
        load(0, k_in.at[0], k_v),
        load(1, v_in.at[0], v_v),
        load(2, q_in.at[0], q_v),
        load(3, gain_in.at[0], gain_v),
        load(4, d_in.at[0], d_v),
    ]
    for c in loads:
        c.start()

    a1 = x * (1 - core) + y * core
    a2 = y * (1 - core) + x * core
    wloads, wsteps = [], []
    for p in (0, 1):
        b1, b2 = rem(a1 + p, 4), rem(a2 + p, 4)

        def dev(c1, c2, p=p):
            o1, o2 = rem(c1 + 4 - p, 4), rem(c2 + 4 - p, 4)
            return (seq, (o1 * 4 + o2) * (1 - core) + (o2 * 4 + o1) * core)

        own32 = w_in.at[pl.ds(pl.multiple_of(core * 64 + p * 32, 32), 32), :]
        wloads.append(load(5 + p, own32, w_g.at[core, p, b1, b2]))
        pair1, pair2 = div(b1, 2) * 2, div(b2, 2) * 2
        for k in (0, 1):
            sub = pl.ds(16 * k, 16)
            own = w_in.at[pl.ds(pl.multiple_of(core * 64 + p * 32 + k * 16, 16), 16), :]
            steps = []

            def add(src, dst, device, base=80 + (p * 2 + k) * 7, steps=steps):
                i = base + len(steps)
                steps.append(
                    pltpu.make_async_remote_copy(
                        src_ref=src, dst_ref=dst, send_sem=ssem.at[i], recv_sem=rsem.at[i],
                        device_id=device, device_id_type=MESH,
                    )
                )

            add(own, w_g.at[core, p, b1, b2, sub], dev(flip(b1), b2))
            two = w_g.at[core, p, pl.ds(pair1, 2), b2, sub]
            add(two, two, dev(3 - b1, b2))
            four = w_g.at[core, p, :, b2, sub]
            add(four, four, dev(b1, flip(b2)))
            eight = w_g.at[core, p, :, pl.ds(pair2, 2), sub]
            add(eight, eight, dev(b1, 3 - b2))
            add(four, four, sib)
            four2 = w_g.at[core, p, :, flip(b2), sub]
            add(four2, four2, sib)
            eight2 = w_g.at[core, p, :, pl.ds(2 - pair2, 2), sub]
            add(eight2, eight2, sib)
            wsteps.append(steps)
    for c in wloads:
        c.start()

    barrier = pltpu.get_barrier_semaphore()
    neighbours = [
        sib,
        (seq, flip(x) * 4 + y), (seq, (3 - x) * 4 + y),
        (seq, x * 4 + flip(y)), (seq, x * 4 + 3 - y),
        (flip(z) * 2 + core, bat), ((3 - z) * 2 + core, bat), (rem(z + 2, 4) * 2 + core, bat),
    ]
    for n in neighbours:
        pl.semaphore_signal(barrier, inc=1, device_id=n, device_id_type=MESH)
    pl.semaphore_wait(barrier, len(neighbours))

    def remote(i, src, dst, device):
        return pltpu.make_async_remote_copy(
            src_ref=src, dst_ref=dst, send_sem=ssem.at[i], recv_sem=rsem.at[i],
            device_id=device, device_id_type=MESH,
        )

    sent = []

    def start(c):
        c.start()
        sent.append(c)

    for k in (0, 1):
        for p in (0, 1):
            start(wsteps[2 * p + k][0])

    dcopy = remote(
        20, d_in.at[0, :, pl.ds(pl.multiple_of((1 - core) * HALF, HALF), HALF)], dosib, sib
    )
    start(dcopy)

    zp1 = (flip(z) * 2 + core, bat)
    zp3 = ((3 - z) * 2 + core, bat)
    zp2 = (rem(z + 2, 4) * 2 + core, bat)
    e0, e1, e2, e3, es, c0, c12, c1, c2, c3, c4 = [[] for _ in range(11)]
    for j in (0, 1):
        four = pl.ds(4 * j, 4)
        n = 51 + 11 * j
        e0.append(remote(n, st.at[:, four], st_sib.at[:, four], sib))
        e1.append(remote(n + 1, cs_send.at[four], r1.at[four], zp1))
        e2.append(remote(n + 2, cs_send.at[four], r2.at[four], zp3))
        e3.append(remote(n + 10, cs_send.at[four], r3.at[four], zp2))
        fars = far.at[core, four, pl.ds(128, 256)]
        es.append(remote(n + 3, fars, fars, sib))
        c0.append(remote(n + 4, gt.at[0, :, four], sg0.at[:, four], sib))
        c12.append(remote(n + 5, gt.at[pl.ds(1, 2), 1 - core, four], recv12.at[:, four], sib))
        c1.append(remote(n + 6, cs12.at[0, four], r1b.at[four], zp1))
        c2.append(remote(n + 7, cs12.at[1, four], r2b.at[four], zp3))
        c3.append(remote(n + 8, cs12.at[1, four], r3b.at[four], zp2))
        sums = sgsum.at[core, four]
        c4.append(remote(n + 9, sums, sums, sib))
    bit = [rem(seq, 2).astype(F32), rem(z, 2).astype(F32), div(z, 2).astype(F32)]

    rot = [rem(z + core, 4), rem(x + core, 4), rem(y + core, 4)]

    def axis_dev(axis, r):
        o = rem(r + 4 - core, 4)
        if axis == 0:
            return (o * 2 + core, bat)
        if axis == 1:
            return (seq, o * 4 + y)
        return (seq, x * 4 + o)

    rs_copies, rs_keeps, rs_kept = [], [], []
    for piece in range(3):
        copies, keeps, local_keeps = [], [], []
        cur = [pl.ds(0, 4)] * 3
        cur_local = [pl.ds(0, 4)] * 3
        for axis in ORDERS[piece]:
            a = rot[axis]
            for sub in (0, 1):
                give, keep = list(cur), list(cur)
                if sub == 0:
                    give[axis] = pl.ds(2 - 2 * div(a, 2), 2)
                    keep[axis] = pl.ds(2 * div(a, 2), 2)
                    to = axis_dev(axis, 3 - a)
                else:
                    give[axis] = pl.ds(flip(a), 1)
                    keep[axis] = pl.ds(a, 1)
                    to = axis_dev(axis, flip(a))
                n = len(copies)
                copies.append(
                    remote(32 + piece * 6 + n, accs[piece].at[tuple(give)], recvs[piece][n], to)
                )
                keeps.append(tuple(keep))
                cur = keep
                if axis == ORDERS[piece][0]:
                    cur_local[axis] = pl.ds(0, 2) if sub == 0 else pl.ds(rem(a, 2), 1)
                else:
                    cur_local[axis] = keep[axis]
                local_keeps.append(tuple(cur_local))
        rs_copies.append(copies)
        rs_keeps.append(keeps)
        rs_kept.append(local_keeps)

    def rs_start(n):
        for piece in range(3):
            start(rs_copies[piece][n])

    def rs_add(n):
        for piece in range(3):
            rs_copies[piece][n].wait_recv()
            keep, local_keep = rs_keeps[piece][n], rs_kept[piece][n]
            recv, acc, f32s = recvs[piece][n], accs[piece], kept[piece]

            def body(i, _, keep=keep, local_keep=local_keep, recv=recv, acc=acc, f32s=f32s):
                at = (keep[0].start + i,) + keep[1:]
                local_at = (local_keep[0].start + i,) + local_keep[1:]
                before = acc[at].astype(F32) if n == 0 else f32s[local_at]
                value = before + recv[i].astype(F32)
                f32s[local_at] = value
                acc[at] = value.astype(BF)
                return 0

            lax.fori_loop(0, keep[0].size, body, 0)

    def hcols(h):
        return pl.ds(pl.multiple_of(h * HD, HD), HD)

    def rolled(h):
        return pltpu.roll(gain_v[...], rem(jnp.int32(HD) - h, HD), 1)

    loads[0].wait()
    loads[1].wait()

    def chunked(i):
        j, r = div(i, 8), rem(i, 8)
        return div(r, 4), 4 * j + rem(r, 4)

    def head(i):
        hi, lo = chunked(i)
        return hi * 8 + lo

    def state_body(i, _):
        hi, lo = chunked(i)
        h = hi * 8 + lo
        kh, vh = k_v[:, hcols(h)], v_v[:, hcols(h)]
        low = dot(kh[:256], vh[:256], 0, 0)
        far[hi, lo, 384:512] = low.astype(BF)
        st[hi, lo] = low + dot(kh[256:], vh[256:], 0, 0)
        return 0

    def ev_w(n, k):
        def event():
            for p in (0, 1):
                steps = wsteps[2 * p + k]
                if n == 1 and k == 0:
                    wloads[p].wait()
                steps[n - 1].wait_recv()
                if n < 4:
                    start(steps[n])
                if n > 1:
                    start(steps[n + 2])

        return event

    def run(body, cuts, count=H, step=1):
        def stepped(i, _):
            for at, *events in cuts:
                if at < count:

                    @pl.when(i * step == at)
                    def _():
                        for event in events:
                            event()

            for j in range(step):
                body(i * step + j, 0)
            return 0

        lax.fori_loop(0, count // step, stepped, 0)
        for at, *events in cuts:
            if at >= count:
                for event in events:
                    event()

    def starts(*copies):
        def event():
            for c in copies:
                start(c)

        return event

    run(
        state_body,
        [(4, ev_w(1, 0)), (8, starts(e0[0]), ev_w(1, 1)), (16, starts(e0[1]))],
        step=2,
    )
    loads[2].wait()
    loads[3].wait()

    rr = lax.broadcasted_iota(jnp.int32, (128, 128), 0)
    cc = lax.broadcasted_iota(jnp.int32, (128, 128), 1)
    same = (rr < 64) == (cc < 64)
    m0 = (rr >= cc) & same
    m1 = (rr >= 64) & (cc < 64)

    def diag_mask(w0, w1):
        return jnp.where(m0, w0, jnp.where(m1, w1, 0.0))

    def ev_e0(j):
        def event():
            e0[j].wait_recv()

            def body(i, _):
                m = 4 * j + i
                for hi in (0, 1):
                    far[hi, m, 0:128] = (st_sib[hi, m] * bit[0]).astype(BF)
                cs_send[m] = (st[core, m] + st_sib[core, m]).astype(BF)
                return 0

            lax.fori_loop(0, 4, body, 0)
            start(e1[j])
            start(e2[j])
            start(e3[j])

        return event

    def ev_e1(j):
        def event():
            e1[j].wait_recv()
            e2[j].wait_recv()
            e3[j].wait_recv()

            def body(i, _):
                m = 4 * j + i
                far[core, m, 128:256] = (r1[m].astype(F32) * bit[1]).astype(BF)
                far[core, m, 256:384] = ((r2[m].astype(F32) + r3[m].astype(F32)) * bit[2]).astype(BF)
                return 0

            lax.fori_loop(0, 4, body, 0)
            start(es[j])

        return event

    def ev_es(j):
        return es[j].wait_recv

    def probs_body(h, _):
        wr = rolled(h)
        scaled = wr * SCALE
        ws = [(scaled if l < 3 else wr)[:, 16 * l : 16 * l + 1] for l in range(7)]
        qh, kh = q_v[:, hcols(h)], k_v[:, hcols(h)]
        for blk in (0, 1):
            r0 = 256 * blk
            sc = dot(qh[r0 : r0 + 256], kh[r0 : r0 + 256], 1, 1)
            a, b = slice(r0, r0 + 128), slice(r0 + 128, r0 + 256)
            probs[h, blk, 0:128, 0:128] = (sc[:128, :128] * diag_mask(ws[0][a], ws[1][a])).astype(BF)
            probs[h, blk, 0:128, 128:256] = jnp.zeros((128, 128), BF)
            probs[h, blk, 128:256, 0:128] = (sc[128:, :128] * ws[2][b]).astype(BF)
            probs[h, blk, 128:256, 128:256] = (
                sc[128:, 128:] * diag_mask(ws[0][b], ws[1][b])
            ).astype(BF)
        qf = qh.astype(F32)
        for b in range(3):
            wq[h, :, 128 * b : 128 * b + 128] = (qf * ws[4 + b]).astype(BF)
        wq[h, 0:256, 384:512] = jnp.zeros((256, 128), BF)
        wq[h, 256:512, 384:512] = (qf[256:] * ws[3][256:]).astype(BF)
        return 0

    run(
        probs_body,
        [
            (1, ev_e0(0)), (2, ev_w(2, 0)), (4, ev_e0(1), ev_w(2, 1)), (11, ev_w(3, 0)),
            (14, ev_e1(0)), (16, ev_w(3, 1), ev_es(0)),
        ],
    )

    def attn_copy(h):
        return pltpu.make_async_remote_copy(
            src_ref=own_v.at[:, hcols(h)], dst_ref=attn_sib.at[h], send_sem=asem.at[h],
            recv_sem=arsem.at[h], device_id=sib, device_id_type=MESH,
        )

    def attn_body(i, _):
        hi, lo = chunked(i)
        h = hi * 8 + lo
        vh = v_v[:, hcols(h)]
        cross = dot(wq[h], far[hi, lo], 1, 0) * SCALE
        for blk in (0, 1):
            r0 = 256 * blk
            out = dot(probs[h, blk], vh[r0 : r0 + 256], 1, 0) + cross[r0 : r0 + 256]
            own_v[r0 : r0 + 256, hcols(h)] = out.astype(BF)
        attn_copy(h).start()
        return 0

    run(attn_body, [(4, ev_e1(1)), (8, ev_es(1)), (16, ev_w(4, 0))], step=2)

    loads[4].wait()
    dcopy.wait_recv()

    def wg_body(i, _):
        h = head(i)
        attn_copy(h).wait_recv()
        own = d_v[:, pl.ds(pl.multiple_of(core * HALF, HALF), HALF)]
        part = dot(own_v[:, hcols(h)], own, 0, 0) + dot(attn_sib[h], dosib[...], 0, 0)
        part = part.astype(BF)
        zd = rem(div(h, 4) + core, 4)
        cd = rem(div(h, 2), 2)
        for xi in (0, 1):
            xd = rem(2 * rem(h, 2) + xi + core, 4)
            for yi in range(4):
                yd = rem(yi + core, 4)
                row = (xi * 4 + yi) * 16
                for piece, (c0_, width) in enumerate(COLS):
                    accs[piece][zd, xd, yd, cd] = part[row : row + 16, c0_ : c0_ + width]
        return 0

    run(wg_body, [(12, ev_w(4, 1))], step=2)
    rs_start(0)

    for steps in wsteps:
        for i in (4, 5, 6):
            steps[i].wait_recv()

    def g_body(i, _):
        blocks = []
        hi, lo = chunked(2 * i)
        for j in (0, 1):
            h = hi * 8 + lo + j
            hx, hy = div(h, 4), rem(h, 4)
            hx1, hy1 = rem(hx + 1, 4), rem(hy + 1, 4)
            blocks += [w_g[0, 0, hx, hy], w_g[0, 1, hx1, hy1], w_g[1, 0, hy, hx], w_g[1, 1, hy1, hx1]]
        weight = jnp.concatenate(blocks, axis=0)
        out = dot(d_v[...], weight, 1, 1).astype(BF)
        for j in (0, 1):
            h = hi * 8 + lo + j
            gh = out[:, 128 * j : 128 * j + 128]
            g_v[h] = gh
            grads = dot(gh, wq[h], 0, 0)
            for b in range(3):
                gt[b, hi, lo + j] = (grads[:, 128 * b : 128 * b + 128] * (bit[b] * SCALE)).astype(BF)
            gt[3, hi, lo + j] = (grads[:, 384:512] * SCALE).astype(BF)
        return 0

    def ev_c12(j):
        def event():
            c12[j].wait_recv()

            def body(i, _):
                m = 4 * j + i
                for b in (0, 1):
                    both = gt[1 + b, core, m].astype(F32) + recv12[b, m].astype(F32)
                    cs12[b, m] = both.astype(BF)
                return 0

            lax.fori_loop(0, 4, body, 0)
            start(c1[j])
            start(c2[j])
            start(c3[j])

        return event

    def ev_c3(j):
        def event():
            c1[j].wait_recv()
            c2[j].wait_recv()
            c3[j].wait_recv()

            def body(i, _):
                m = 4 * j + i
                both = r1b[m].astype(F32) + r2b[m].astype(F32) + r3b[m].astype(F32)
                sgsum[core, m] = both.astype(BF)
                return 0

            lax.fori_loop(0, 4, body, 0)
            start(c4[j])

        return event

    run(
        g_body,
        [(4, starts(c0[0], c12[0])), (6, ev_c12(0)), (8, starts(c0[1], c12[1]))],
        count=H // 2,
    )

    def ev_rs(n):
        def event():
            rs_add(n)
            rs_start(n + 1)

        return event

    def wait_attn(h, _):
        attn_copy(h).wait_send()
        return 0

    lax.fori_loop(0, H, wait_attn, 0)
    tacc[...] = jnp.zeros_like(tacc)
    dsel = lax.broadcasted_iota(jnp.int32, (256, 128), 1) - 16 * div(
        lax.broadcasted_iota(jnp.int32, (256, 128), 0), 64
    )
    frow = lax.broadcasted_iota(jnp.int32, (512, 128), 0)
    dfar = lax.broadcasted_iota(jnp.int32, (512, 128), 1) - 64 - 16 * div(frow, 128)

    def dq_body(h, _):
        wr = rolled(h)
        ws = [wr[:, 16 * l : 16 * l + 1] for l in range(7)]
        qf = q_v[:, hcols(h)].astype(F32)
        kh, vh, gh = k_v[:, hcols(h)], v_v[:, hcols(h)], g_v[h]
        fh = far.at[div(h, 8), rem(h, 8)]
        sel = (dsel == h).astype(F32).astype(BF)
        fsel = (dfar == h).astype(F32).astype(BF)
        dq = None
        prods = []
        for b in range(3):
            if b % 2 == 0:
                pair = dot(gh, fh[128 * b : 128 * b + 256], 1, 1)
            pb = pair[:, 128 * (b % 2) : 128 * (b % 2) + 128]
            prods.append((qf * pb).astype(BF))
            term = pb * ws[4 + b]
            dq = term if dq is None else dq + term
        p3 = pair[256:, 128:]
        prod3 = (qf[256:] * p3).astype(BF)
        p3 = p3 * ws[3][256:]
        far_sums = []
        for blk in (0, 1):
            r0 = 256 * blk
            fars = [prods[b][r0 : r0 + 256] for b in range(3)]
            if blk == 1:
                fars.append(prod3)
                sums = dot(jnp.concatenate(fars, axis=1), fsel, 1, 0)
            else:
                sums = dot(jnp.concatenate(fars, axis=1), fsel[:384], 1, 0)
            far_sums.append(sums)
        for t in range(4):
            blk, r0, c0_ = t // 2, 128 * t, 256 * (t // 2)
            rows, inner = slice(r0, r0 + 128), slice(r0 - c0_, r0 - c0_ + 128)
            width = r0 - c0_ + 128
            pg = dot(gh[rows], vh[c0_ : r0 + 128], 1, 1)
            sg = (pg[:, -128:] * diag_mask(ws[0][rows], ws[1][rows])).astype(BF)
            if t % 2 == 1:
                sg = jnp.concatenate([(pg[:, :128] * ws[2][rows]).astype(BF), sg], axis=1)
            wq[h, rows, 0:width] = sg
            energy = (pg * probs[h, blk, inner, 0:width].astype(F32)).astype(BF)
            out = dot(sg, kh[c0_ : r0 + 128], 1, 0) + dq[rows]
            if blk == 1:
                out = out + p3[inner]
            own_v[rows, hcols(h)] = (out * SCALE).astype(BF)
            tacc[rows] += far_sums[blk][inner] + dot(energy, sel[:width], 1, 0)
        return 0

    run(
        dq_body,
        [
            (2, ev_rs(0)), (3, ev_c12(1)), (6, ev_c3(0)), (8, ev_rs(1)), (13, ev_rs(2)), (16, ev_c3(1), ev_rs(3)),
        ],
    )
    for j in (0, 1):
        c0[j].wait_recv()
        c4[j].wait_recv()

    def dk_body(h, _):
        hi, lo = div(h, 8), rem(h, 8)
        base = sg0[hi, lo].astype(F32) + sgsum[hi, lo].astype(F32)
        halves = ((base + gt[3, hi, lo].astype(F32)).astype(BF), base.astype(BF))
        for blk in (0, 1):
            for r0 in (256 * blk, 256 * blk + 128):
                rows, after = slice(r0, r0 + 128), slice(r0, 256 * blk + 256)
                inner = slice(r0 - 256 * blk, r0 - 256 * blk + 128)
                kb, vb = k_v[rows, hcols(h)], v_v[rows, hcols(h)]
                dv = dot(probs[h, blk, inner.start : 256, inner], g_v[h, after], 0, 0)
                dk = dot(wq[h, after, inner], q_v[after, hcols(h)], 0, 0)
                k_v[rows, hcols(h)] = (dk * SCALE + dot(vb, halves[blk], 1, 0)).astype(BF)
                v_v[rows, hcols(h)] = (dv + dot(kb, halves[blk], 1, 1)).astype(BF)
        return 0

    def finish():
        for piece, (first, width) in enumerate(COLS):
            rs_copies[piece][5].wait_recv()
            f32s, recv = kept[piece], recvs[piece][5]
            at = tuple(s.start for s in rs_kept[piece][5])
            cols = slice(first, first + width)
            wgout[core, :, cols] = f32s[at + (core,)] + recv[0, 0, 0, core].astype(F32)
            finsend[:, cols] = f32s[at + (1 - core,)] + recv[0, 0, 0, 1 - core].astype(F32)
        start(last)

    last = remote(50, finsend, wgout.at[core], sib)
    run(dk_body, [(6, ev_rs(4)), (14, finish)], step=2)

    lane = lax.broadcasted_iota(jnp.int32, (64, 128), 1)
    for i in range(8):
        rows = slice(64 * i, 64 * i + 64)
        g4 = i % 4
        t = tacc[rows]

        def moved(frm, to, t=t):
            shift = (to - frm) * 16 % 128
            return pltpu.roll(t, shift, 1) if shift else t

        res = jnp.where(lane < 16, moved(g4, 0), 0.0)
        if g4 % 2 == 1:
            res = jnp.where((lane >= 16) & (lane < 32), moved(g4 - 1, 1), res)
        if g4 >= 2:
            res = jnp.where((lane >= 32) & (lane < 48), moved(0, 2) + moved(1, 2), res)
        res = res / gain_v[rows]
        if i >= 4:
            res = jnp.where((lane >= 48) & (lane < 64), moved(7, 3) * SCALE, res)
        res = jnp.where((lane >= 64) & (lane < 112), t * SCALE, res)
        tacc[rows] = res
    last.wait_recv()
    for i in (0, 1):
        wg_out[:, HALF * i : HALF * i + HALF] = wgout[i]
    for c in sent:
        c.wait_send()


def local(queries, keys, values, level_gain, out_weight, out_grad):
    big = pltpu.VMEM((1, T, D), BF)
    state = (2, 8, HD, HD)
    scratch = [
        pltpu.VMEM((T, D), BF),
        pltpu.VMEM((T, D), BF),
        pltpu.VMEM((T, HD), F32),
        pltpu.VMEM((2, 2, 4, 4, 32, D), BF),
        pltpu.VMEM((H, T, HD), BF),
        pltpu.VMEM((T, HALF), BF),
        pltpu.VMEM((H, T, T), BF),
        pltpu.VMEM((H, 2, 256, 256), BF),
        pltpu.VMEM((H, T, HD), BF),
        pltpu.VMEM((2, 8, T, HD), BF),
        pltpu.VMEM(state, F32),
        pltpu.VMEM(state, F32),
        pltpu.VMEM((8, HD, HD), BF),
        pltpu.VMEM((8, HD, HD), BF),
        pltpu.VMEM((8, HD, HD), BF),
        pltpu.VMEM((8, HD, HD), BF),
        pltpu.VMEM((4,) + state, BF),
        pltpu.VMEM(state, BF),
        pltpu.VMEM(state, BF),
        pltpu.VMEM(state, BF),
        pltpu.VMEM((8, HD, HD), BF),
        pltpu.VMEM((8, HD, HD), BF),
        pltpu.VMEM((8, HD, HD), BF),
        pltpu.VMEM(state, BF),
        pltpu.VMEM((2, 16, HALF), F32),
        pltpu.VMEM((16, HALF), F32),
    ]
    scratch += [pltpu.VMEM((4, 4, 4, 2, 16, width), BF) for _, width in COLS]
    scratch += [pltpu.VMEM(shape, F32) for shape in recv_shapes()[::6]]
    scratch += [pltpu.VMEM(shape, BF) for shape in recv_shapes()]
    scratch += [
        pltpu.SemaphoreType.DMA((8,)),
        pltpu.SemaphoreType.DMA((112,)),
        pltpu.SemaphoreType.DMA((112,)),
        pltpu.SemaphoreType.DMA((H,)),
        pltpu.SemaphoreType.DMA((H,)),
    ]
    anyspace = pl.BlockSpec(memory_space=pl.ANY)
    return pl.pallas_call(
        kernel,
        out_shape=(
            big, big, big,
            pltpu.VMEM((1, T, HD), F32),
            pltpu.VMEM((16, D), F32),
        ),
        in_specs=[anyspace] * 6,
        out_specs=(pl.BlockSpec(memory_space=pltpu.VMEM),) * 5,
        scratch_shapes=scratch,
        compiler_params=pltpu.CompilerParams(
            collective_id=0, has_side_effects=True, vmem_limit_bytes=57 * 2**20
        ),
        cost_estimate=pl.CostEstimate(flops=20 * 10**9, bytes_accessed=16 * 2**20, transcendentals=0),
    )(queries, keys, values, level_gain, out_weight, out_grad)


def solution(mesh):
    tokens = P("batch", "seq", None)
    return jax.shard_map(
        local,
        mesh=mesh,
        in_specs=(tokens, tokens, tokens, tokens, P("batch", None), tokens),
        out_specs=(tokens, tokens, tokens, tokens, P(("seq", "batch"), None)),
        check_vma=False,
    )
```
